512 devices in a mesh: inter: 16 (over z), intra: 32 (over y, x, core).
Axes of the slice: x: 4, y: 4, z: 16, core: 2. Of those that a mesh axis runs over, the one named last changes fastest.
Arguments:
- tokens: bfloat16 [65536, 768], P(('inter', 'intra')), may hold values from -6 to 6
- expert_ids: int32 [65536], P(('inter', 'intra')), may hold values from 0 to 63
- slot_ids: int32 [65536], P(('inter', 'intra')), may hold values from 0 to 1, as said below
- keep_mask: int32 [65536], P(('inter', 'intra')), may hold values from 0 to 1, as said below
- gate_prob: float32 [65536], P(('inter', 'intra')), may hold values from 0.25 to 1
- out_grad: bfloat16 [65536, 768], P(('inter', 'intra')), may hold values from -1.5 to 1.5
- in_weight: bfloat16 [16, 32, 768, 384], P('inter', 'intra'), may hold values from -0.21875 to 0.21875
- out_weight: bfloat16 [16, 32, 384, 768], P('inter', 'intra'), may hold values from -0.109375 to 0.109375
Outputs:
- expert_out: bfloat16 [65536, 768], P(('inter', 'intra'))
- gate_grad: float32 [65536], P(('inter', 'intra'))
- token_grad: bfloat16 [65536, 768], P(('inter', 'intra'))
- in_weight_grad: bfloat16 [16, 32, 768, 384], P('inter', 'intra')
- out_weight_grad: bfloat16 [16, 32, 384, 768], P('inter', 'intra')
The draws below stay inside these ranges and needn't reach their ends.
Inputs may be any that keep to these rules, and one draw needn't show every extreme that they name: `slot_ids`: within the rows of one device, a token's slot is the number of earlier tokens of that device with the same expert, capped at 1; kept tokens of one device have distinct expert and slot pairs. One expert has more than 2 tokens in the rows of every device. `keep_mask`: 1 exactly where fewer than 2 earlier tokens of the same device chose the same expert.
All inputs are finite; a program needn't handle non-finite values.
Results may differ from the reference program's by a relative error of at most 0.0064.
Values may be sent and summed in bfloat16 or wider, within the bound.
No kernel may reach another device: no remote copies, remote signals or barrier semaphores. Data moves between devices by JAX's collectives and lax.ppermute only.
A program may use at most 64 MiB of HBM per device.

```python
import math
import jax
import jax.numpy as jnp
from jax import lax

D = 768
FF = 3072
EGRP = 2
TOK_DEV = 128
FSPLIT = 8
FF_DEV = 384
EXPERTS = 64
CAP = 2
TOKENS = 65536
N_INTER = 16
N_INTRA = 32


def routing(key):
    key_drawn, key_popular, key_choose, key_hot, key_offsets = jax.random.split(key, 5)
    blocks = TOKENS // TOK_DEV
    uniform_ids = jax.random.randint(key_drawn, (TOKENS,), 0, EXPERTS)
    popular = jax.random.randint(key_popular, (TOKENS,), 0, 4)
    choose = jax.random.randint(key_choose, (TOKENS,), 0, 8)
    hot_expert = jax.random.randint(key_hot, (), 0, EXPERTS)
    chosen = jnp.where(choose == 0, (hot_expert + popular) % EXPERTS, uniform_ids)
    position = jnp.arange(TOKENS) % TOK_DEV
    offsets = jnp.repeat(jax.random.randint(key_offsets, (blocks,), 0, TOK_DEV - CAP), TOK_DEV)
    forced = (position >= offsets) & (position <= offsets + CAP)
    chosen = jnp.where(forced, hot_expert, chosen).astype(jnp.int32)
    onehot = (chosen.reshape(blocks, TOK_DEV)[:, :, None] == jnp.arange(EXPERTS)[None, None, :]).astype(jnp.int32)
    earlier = jnp.cumsum(onehot, axis=1) - onehot
    rank_in = jnp.sum(earlier * onehot, axis=2).reshape(TOKENS)
    slots = jnp.minimum(rank_in, CAP - 1).astype(jnp.int32)
    kept = (rank_in < CAP).astype(jnp.int32)
    return (chosen, slots, kept)


def draw_expert_ids(key, part):
    shared = routing(key)
    return shared[0]


def draw_slot_ids(key, part):
    shared = routing(key)
    return shared[1]


def draw_keep_mask(key, part):
    shared = routing(key)
    return shared[2]


def level_of(rng, extent, cuts, least, high):
    gain = 1.0
    for dim, blocks in cuts:
        draws = jax.random.uniform(jax.random.fold_in(jax.random.fold_in(rng, 6), dim), (blocks,), jnp.float32, least / len(cuts), high / len(cuts))
        gain = gain * jnp.repeat(jnp.exp(draws), extent[dim] // blocks).reshape((-1,) + (1,) * (len(extent) - 1 - dim))
    return gain


def scatter_about(own_key, shape, width, limit, cuts=(), dtype=jnp.bfloat16):
    factor_of = level_of(own_key, shape, cuts, -0.22, 0.18) if cuts else 1.0
    drawn = jax.random.normal(own_key, shape, jnp.float32) * width * factor_of
    return jnp.minimum(jnp.maximum(drawn, -limit), limit).astype(dtype)


def setup_inputs(seed: int = 0) -> dict:
    seeds = jax.random.split(jax.random.key(seed), 9)
    tokens = scatter_about(seeds[0], (TOKENS, D), 1.0, 6.0, ((0, 512),))
    expert_ids = draw_expert_ids(jax.random.fold_in(seeds[8], 71), 0)
    slot_ids = draw_slot_ids(jax.random.fold_in(seeds[8], 71), 0)
    keep_mask = draw_keep_mask(jax.random.fold_in(seeds[8], 71), 0)
    gate_prob = jnp.clip(0.25 + 0.75 * jax.random.uniform(seeds[4], (TOKENS,), jnp.float32) ** level_of(seeds[4], (TOKENS,), ((0, 512),), -0.2, 0.2), 0.25, 1.0)
    out_grad = scatter_about(seeds[5], (TOKENS, D), 0.25, 1.5, ((0, 512),))
    in_weight = scatter_about(seeds[6], (N_INTER, N_INTRA, D, FF_DEV), D ** -0.5, 0.21875, ((0, 16), (1, 32)))
    out_weight = scatter_about(seeds[7], (N_INTER, N_INTRA, FF_DEV, D), FF ** -0.5, 0.109375, ((0, 16), (1, 32)))
    return {"tokens": tokens, "expert_ids": expert_ids, "slot_ids": slot_ids, "keep_mask": keep_mask, "gate_prob": gate_prob, "out_grad": out_grad, "in_weight": in_weight, "out_weight": out_weight}


gelu_root = math.sqrt(2.0 / math.pi)
gelu_cubic = 0.044715

def gelu(pre_value):
    argument = gelu_root * (pre_value + gelu_cubic * pre_value * pre_value * pre_value)
    return 0.5 * pre_value * (1.0 + jnp.tanh(argument))

def gelu_slope(pre_value):
    argument = gelu_root * (pre_value + gelu_cubic * pre_value * pre_value * pre_value)
    slope_tanh = jnp.tanh(argument)
    return 0.5 * (1.0 + slope_tanh) + 0.5 * pre_value * (1.0 - slope_tanh * slope_tanh) * gelu_root * (1.0 + 3.0 * gelu_cubic * pre_value * pre_value)

def rounded_sum(pieces):
    rounded = lax.optimization_barrier(pieces.astype(jnp.bfloat16))
    return lax.optimization_barrier(jnp.sum(rounded.astype(jnp.float32), axis=0)).astype(jnp.bfloat16)

def per_expert(items):
    slot_x, slot_g, weight_in, weight_out = items
    row_count = slot_x.shape[0]
    pre_act = jnp.dot(slot_x, weight_in, preferred_element_type=jnp.float32)
    hidden = gelu(pre_act).astype(jnp.bfloat16)
    pieces = jnp.einsum('rkf,kfd->krd', hidden.reshape(row_count, FSPLIT, FF_DEV).astype(jnp.float32), weight_out.reshape(FSPLIT, FF_DEV, D).astype(jnp.float32))
    ffn_out = rounded_sum(pieces)
    hidden_grad = jnp.dot(slot_g, weight_out.T, preferred_element_type=jnp.float32)
    pre_grad = (hidden_grad * gelu_slope(pre_act)).astype(jnp.bfloat16)
    out_grad_w = jnp.dot(hidden.T, slot_g, preferred_element_type=jnp.float32).astype(jnp.bfloat16)
    in_grad_w = jnp.dot(slot_x.T, pre_grad, preferred_element_type=jnp.float32).astype(jnp.bfloat16)
    back_pieces = jnp.einsum('rkf,dkf->krd', pre_grad.reshape(row_count, FSPLIT, FF_DEV).astype(jnp.float32), weight_in.reshape(D, FSPLIT, FF_DEV).astype(jnp.float32))
    input_grad = rounded_sum(back_pieces)
    return (ffn_out, input_grad, in_grad_w, out_grad_w)

def reference(tokens, expert_ids, slot_ids, keep_mask, gate_prob, out_grad, in_weight, out_weight):
    blocks = TOKENS // TOK_DEV
    block_of = (jnp.arange(TOKENS) // TOK_DEV).astype(jnp.int32)
    keep_float = keep_mask.astype(jnp.float32)
    whole_in = jnp.transpose(in_weight.reshape(EGRP, FSPLIT, N_INTRA, D, FF_DEV), (0, 2, 3, 1, 4)).reshape(EXPERTS, D, FF)
    whole_out = jnp.transpose(out_weight.reshape(EGRP, FSPLIT, N_INTRA, FF_DEV, D), (0, 2, 1, 3, 4)).reshape(EXPERTS, FF, D)

    def place_rows(values):
        buffer = jnp.zeros((blocks, EXPERTS, CAP, D), jnp.float32)
        return buffer.at[block_of, expert_ids, slot_ids].add(values * keep_float[:, None])

    def pick_rows(buffer):
        return buffer[block_of, expert_ids, slot_ids].astype(jnp.float32) * keep_float[:, None]

    def by_expert(buffer):
        return jnp.transpose(buffer, (1, 0, 2, 3)).reshape(EXPERTS, blocks * CAP, D)

    def by_block(stacked):
        return jnp.transpose(stacked.reshape(EXPERTS, blocks, CAP, D), (1, 0, 2, 3))
    dispatched = place_rows(tokens.astype(jnp.float32)).astype(jnp.bfloat16)
    scaled_grad = lax.optimization_barrier((gate_prob[:, None] * out_grad.astype(jnp.float32)).astype(jnp.bfloat16))
    slot_grad = place_rows(scaled_grad.astype(jnp.float32)).astype(jnp.bfloat16)
    ffn_out, input_grad, in_grad_whole, out_grad_whole = lax.map(per_expert, (by_expert(dispatched), by_expert(slot_grad), whole_in, whole_out))
    ffn_tok = pick_rows(by_block(ffn_out))
    expert_out = (gate_prob[:, None] * ffn_tok).astype(jnp.bfloat16)
    gate_grad = lax.optimization_barrier(jnp.sum(out_grad.astype(jnp.float32) * ffn_tok, axis=1))
    token_grad = pick_rows(by_block(input_grad)).astype(jnp.bfloat16)
    in_weight_grad = jnp.transpose(in_grad_whole.reshape(EGRP, N_INTRA, D, FSPLIT, FF_DEV), (0, 3, 1, 2, 4)).reshape(N_INTER, N_INTRA, D, FF_DEV)
    out_weight_grad = jnp.transpose(out_grad_whole.reshape(EGRP, N_INTRA, FSPLIT, FF_DEV, D), (0, 2, 1, 3, 4)).reshape(N_INTER, N_INTRA, FF_DEV, D)
    return (expert_out, gate_grad, token_grad, in_weight_grad, out_weight_grad)
```

```python
import math

import jax
import jax.numpy as jnp
from jax import lax
from jax.sharding import PartitionSpec as P

EGRP = 2


gelu_root = math.sqrt(2.0 / math.pi)
gelu_cubic = 0.044715


def gelu_and_slope(pre_value):
    square = pre_value * pre_value
    argument = gelu_root * (pre_value + gelu_cubic * square * pre_value)
    slope_tanh = jnp.tanh(argument)
    half_up = 0.5 * (1.0 + slope_tanh)
    value = pre_value * half_up
    slope = half_up + 0.5 * pre_value * (1.0 - slope_tanh * slope_tanh) * gelu_root * (
        1.0 + 3.0 * gelu_cubic * square
    )
    return value, slope


def on_device(tokens, expert_ids, slot_ids, keep_mask, gate_prob, out_grad, in_weight, out_weight):
    tok_rows, model_width = tokens.shape
    intra_size = lax.axis_size("intra")
    inter_size = lax.axis_size("inter")
    blocks_ff = inter_size // EGRP
    experts = EGRP * intra_size
    capacity = max(2, tok_rows * 5 // 4 // experts)
    my_group = lax.axis_index("inter") // blocks_ff
    weight_in = in_weight[0, 0]
    weight_out = out_weight[0, 0]
    rows_one = intra_size * capacity
    columns = expert_ids * capacity + slot_ids
    one_hot = (
        (columns[:, None] == jnp.arange(experts * capacity)[None, :]) & (keep_mask[:, None] == 1)
    ).astype(jnp.bfloat16)

    scaled_grad = (gate_prob[:, None] * out_grad.astype(jnp.float32)).astype(jnp.bfloat16)
    both = jnp.concatenate([tokens, scaled_grad], axis=1)
    placed = jnp.einsum("tc,td->cd", one_hot, both, preferred_element_type=jnp.float32).astype(jnp.bfloat16)
    placed = placed.reshape(EGRP, intra_size, capacity, 2 * model_width)
    moved = lax.all_to_all(placed, "intra", split_axis=1, concat_axis=1, tiled=True)
    moved = moved.reshape(1, EGRP, rows_one, 2 * model_width)
    spread = lax.all_gather(moved, "inter", axis=0, tiled=True)
    mine = lax.dynamic_index_in_dim(spread, my_group, axis=1, keepdims=False)
    mine = mine.reshape(inter_size * rows_one, 2 * model_width)
    rows_x, rows_g = mine[:, :model_width], mine[:, model_width:]

    pre_act = jnp.dot(rows_x, weight_in, preferred_element_type=jnp.float32)
    hidden, slope = gelu_and_slope(pre_act)
    hidden = hidden.astype(jnp.bfloat16)
    partial_out = jnp.dot(hidden, weight_out, preferred_element_type=jnp.float32).astype(jnp.bfloat16)
    hidden_grad = jnp.einsum("rd,fd->rf", rows_g, weight_out, preferred_element_type=jnp.float32)
    pre_grad = (hidden_grad * slope).astype(jnp.bfloat16)
    partial_in = jnp.einsum("rf,df->rd", pre_grad, weight_in, preferred_element_type=jnp.float32).astype(jnp.bfloat16)
    partial = jnp.concatenate([partial_out, partial_in], axis=1).reshape(inter_size, 1, rows_one, 2 * model_width)
    which = jnp.arange(EGRP)[None, :, None, None] == my_group
    send = jnp.where(which, partial, jnp.zeros((), jnp.bfloat16))
    summed = lax.psum_scatter(send, "inter", scatter_dimension=0, tiled=True)

    out_weight_grad = jnp.einsum("rf,rd->fd", hidden, rows_g, preferred_element_type=jnp.float32).astype(jnp.bfloat16)
    in_weight_grad = jnp.einsum("rd,rf->df", rows_x, pre_grad, preferred_element_type=jnp.float32).astype(jnp.bfloat16)

    home = lax.all_to_all(
        summed.reshape(EGRP, intra_size, capacity, 2 * model_width), "intra", split_axis=1, concat_axis=1, tiled=True
    )
    home = home.reshape(experts * capacity, 2 * model_width)
    picked = jnp.dot(one_hot, home, preferred_element_type=jnp.float32)
    ffn_tok = picked[:, :model_width]
    expert_out = (gate_prob[:, None] * ffn_tok).astype(jnp.bfloat16)
    gate_grad = jnp.sum(out_grad.astype(jnp.float32) * ffn_tok, axis=1)
    token_grad = picked[:, model_width:].astype(jnp.bfloat16)
    return (
        expert_out,
        gate_grad,
        token_grad,
        in_weight_grad[None, None],
        out_weight_grad[None, None],
    )


def solution(mesh):
    tok = P(("inter", "intra"), None)
    per = P(("inter", "intra"))
    wgt = P("inter", "intra", None, None)
    return jax.shard_map(
        on_device,
        mesh=mesh,
        in_specs=(tok, per, per, per, per, tok, wgt, wgt),
        out_specs=(tok, per, tok, wgt, wgt),
        check_vma=False,
    )
```

```python
import functools
import math

import jax
import jax.numpy as jnp
from jax import lax
from jax.experimental import pallas as pl
from jax.experimental.pallas import tpu as pltpu
from jax.sharding import PartitionSpec as P

EGRP = 2
CAP = 2
KINDS = 2
TILE = EGRP * KINDS * CAP
VMEM_BYTES = 48 * 1024 * 1024

gelu_root = math.sqrt(2.0 / math.pi)
gelu_cubic = 0.044715


def gelu_and_slope(pre_value):
    square = pre_value * pre_value
    argument = gelu_root * (pre_value + gelu_cubic * square * pre_value)
    slope_tanh = jnp.tanh(argument)
    half_up = 0.5 * (1.0 + slope_tanh)
    value = pre_value * half_up
    slope = half_up + 0.5 * pre_value * (1.0 - slope_tanh * slope_tanh) * gelu_root * (
        1.0 + 3.0 * gelu_cubic * square
    )
    return value, slope


def dot(left, right, dims=((1,), (0,))):
    return lax.dot_general(left, right, (dims, ((), ())), preferred_element_type=jnp.float32)


def slot_row(experts, slots, keep, intra_size):
    group = (experts >= intra_size).astype(jnp.int32)
    row = (experts - group * intra_size) * TILE + group * (KINDS * CAP) + slots
    return jnp.where(keep == 1, row, -TILE)


def as_column(row):
    count = row.shape[1]
    shape = (count, count)
    diagonal = lax.broadcasted_iota(jnp.int32, shape, 0) == lax.broadcasted_iota(jnp.int32, shape, 1)
    return jnp.sum(jnp.where(diagonal, row, 0.0), axis=1, keepdims=True)


def as_row(column):
    count = column.shape[0]
    shape = (count, count)
    diagonal = lax.broadcasted_iota(jnp.int32, shape, 0) == lax.broadcasted_iota(jnp.int32, shape, 1)
    return jnp.sum(jnp.where(diagonal, column, 0.0), axis=0, keepdims=True)


def place_kernel(intra_size, tokens, experts, slots, keep, gate, out_grad, send):
    count = tokens.shape[0]
    row = slot_row(experts[...], slots[...], keep[...], intra_size)
    scaled = (as_column(gate[...]) * out_grad[...].astype(jnp.float32)).astype(jnp.bfloat16)
    at = lax.broadcasted_iota(jnp.int32, (send.shape[0], count), 0)
    hot_x = (at == row).astype(jnp.bfloat16)
    hot_g = (at == row + CAP).astype(jnp.bfloat16)
    send[...] = (dot(hot_x, tokens[...]) + dot(hot_g, scaled)).astype(jnp.bfloat16)


def pick_kernel(intra_size, home, experts, slots, keep, gate, out_grad, expert_out, gate_grad, token_grad):
    count = out_grad.shape[0]
    row = slot_row(experts[...], slots[...], keep[...], intra_size)
    row = as_column(row.astype(jnp.float32)).astype(jnp.int32)
    at = lax.broadcasted_iota(jnp.int32, (count, home.shape[0]), 1)
    ffn_tok = dot((at == row).astype(jnp.bfloat16), home[...])
    expert_out[...] = (as_column(gate[...]) * ffn_tok).astype(jnp.bfloat16)
    gate_grad[...] = as_row(jnp.sum(out_grad[...].astype(jnp.float32) * ffn_tok, axis=1, keepdims=True))
    token_grad[...] = dot((at == row + CAP).astype(jnp.bfloat16), home[...]).astype(jnp.bfloat16)


def expert_kernel(group_ref, rows, weight_in, weight_out, send, rows_x, rows_g, hidden, pre_grad):
    sources, wide, _ = rows.shape
    narrow = wide // EGRP
    half = narrow // KINDS
    first = group_ref[0] * (KINDS * CAP)

    def place_of(index):
        kind = (index >= half).astype(jnp.int32)
        within = index - kind * half
        return (within >> 1) * TILE + first + kind * CAP + (within & 1)

    shape = (narrow, wide)
    take = (
        lax.broadcasted_iota(jnp.int32, shape, 1) == place_of(lax.broadcasted_iota(jnp.int32, shape, 0))
    ).astype(jnp.bfloat16)
    shape = (wide, narrow)
    put = (
        lax.broadcasted_iota(jnp.int32, shape, 0) == place_of(lax.broadcasted_iota(jnp.int32, shape, 1))
    ).astype(jnp.bfloat16)
    for s in range(sources):
        taken = dot(take, rows[s]).astype(jnp.bfloat16)
        rows_x[pl.ds(s * half, half), :] = taken[:half]
        rows_g[pl.ds(s * half, half), :] = taken[half:]
    pre_act = dot(rows_x[...], weight_in[...])
    hidden_grad = dot(rows_g[...], weight_out[...], ((1,), (1,)))
    value, slope = gelu_and_slope(pre_act)
    hidden[...] = value.astype(jnp.bfloat16)
    pre_grad[...] = (hidden_grad * slope).astype(jnp.bfloat16)
    part_out = dot(hidden[...], weight_out[...]).astype(jnp.bfloat16)
    part_in = dot(pre_grad[...], weight_in[...], ((1,), (1,))).astype(jnp.bfloat16)
    for s in range(sources):
        both = jnp.concatenate([part_out[s * half : (s + 1) * half], part_in[s * half : (s + 1) * half]], axis=0)
        send[s] = dot(put, both).astype(jnp.bfloat16)


def on_device(tokens, expert_ids, slot_ids, keep_mask, gate_prob, out_grad, in_weight, out_weight):
    tok_rows, width = tokens.shape
    intra_size = lax.axis_size("intra")
    inter_size = lax.axis_size("inter")
    blocks_ff = inter_size // EGRP
    group = (lax.axis_index("inter") // blocks_ff).astype(jnp.int32).reshape(1)
    weight_in = in_weight[0, 0]
    weight_out = out_weight[0, 0]
    hidden_units = weight_in.shape[1]
    wide = intra_size * TILE
    params = pltpu.CompilerParams(vmem_limit_bytes=VMEM_BYTES)
    routing = (expert_ids[None], slot_ids[None], keep_mask[None], gate_prob[None])

    placed = pl.pallas_call(
        functools.partial(place_kernel, intra_size),
        out_shape=jax.ShapeDtypeStruct((wide, width), jnp.bfloat16),
        compiler_params=params,
        name="place",
    )(tokens, *routing, out_grad)
    moved = lax.all_to_all(placed.reshape(intra_size, TILE, width), "intra", 0, 0, tiled=True)
    spread = lax.all_gather(moved.reshape(1, wide, width), "inter", axis=0, tiled=True)

    step = 4
    rows_step = step * wide // (EGRP * KINDS)
    rows_all = inter_size * wide // (EGRP * KINDS)
    whole = lambda i, *_: (0, 0)
    by_row = lambda i, *_: (i, 0)
    send, rows_x, rows_g, hidden, pre_grad = pl.pallas_call(
        expert_kernel,
        grid_spec=pltpu.PrefetchScalarGridSpec(
            num_scalar_prefetch=1,
            grid=(inter_size // step,),
            in_specs=[
                pl.BlockSpec((step, wide, width), lambda i, *_: (i, 0, 0)),
                pl.BlockSpec((width, hidden_units), whole),
                pl.BlockSpec((hidden_units, width), whole),
            ],
            out_specs=[
                pl.BlockSpec((step, wide, width), lambda i, *_: (i, 0, 0)),
                pl.BlockSpec((rows_step, width), by_row),
                pl.BlockSpec((rows_step, width), by_row),
                pl.BlockSpec((rows_step, hidden_units), by_row),
                pl.BlockSpec((rows_step, hidden_units), by_row),
            ],
        ),
        out_shape=[
            jax.ShapeDtypeStruct((inter_size, wide, width), jnp.bfloat16),
            jax.ShapeDtypeStruct((rows_all, width), jnp.bfloat16),
            jax.ShapeDtypeStruct((rows_all, width), jnp.bfloat16),
            jax.ShapeDtypeStruct((rows_all, hidden_units), jnp.bfloat16),
            jax.ShapeDtypeStruct((rows_all, hidden_units), jnp.bfloat16),
        ],
        compiler_params=params,
        name="expert",
    )(group, spread, weight_in, weight_out)
    summed = lax.psum_scatter(send, "inter", scatter_dimension=0, tiled=True)

    out_weight_grad = dot(hidden, rows_g, ((0,), (0,))).astype(jnp.bfloat16)
    in_weight_grad = dot(rows_x, pre_grad, ((0,), (0,))).astype(jnp.bfloat16)
    summed, out_weight_grad, in_weight_grad = lax.optimization_barrier((summed, out_weight_grad, in_weight_grad))

    home = lax.all_to_all(summed.reshape(intra_size, TILE, width), "intra", 0, 0, tiled=True)
    expert_out, gate_grad, token_grad = pl.pallas_call(
        functools.partial(pick_kernel, intra_size),
        out_shape=[
            jax.ShapeDtypeStruct((tok_rows, width), jnp.bfloat16),
            jax.ShapeDtypeStruct((1, tok_rows), jnp.float32),
            jax.ShapeDtypeStruct((tok_rows, width), jnp.bfloat16),
        ],
        compiler_params=params,
        name="pick",
    )(home.reshape(wide, width), *routing, out_grad)
    return (
        expert_out,
        gate_grad.reshape(tok_rows),
        token_grad,
        in_weight_grad[None, None],
        out_weight_grad[None, None],
    )


def solution(mesh):
    tok = P(("inter", "intra"), None)
    per = P(("inter", "intra"))
    wgt = P("inter", "intra", None, None)
    return jax.shard_map(
        on_device,
        mesh=mesh,
        in_specs=(tok, per, per, per, per, tok, wgt, wgt),
        out_specs=(tok, per, tok, wgt, wgt),
        check_vma=False,
    )
```

```python
import functools
import math

import jax
import jax.numpy as jnp
from jax import lax
from jax.experimental import pallas as pl
from jax.experimental.pallas import tpu as pltpu
from jax.sharding import PartitionSpec as P

EGRP = 2
CAP = 2
KINDS = 2
TILE = EGRP * KINDS * CAP
VMEM_BYTES = 60 * 1024 * 1024

gelu_root = math.sqrt(2.0 / math.pi)
gelu_cubic = 0.044715


def gelu_and_slope(pre_value):
    square = pre_value * pre_value
    argument = gelu_root * (pre_value + gelu_cubic * square * pre_value)
    slope_tanh = jnp.tanh(argument)
    half_up = 0.5 * (1.0 + slope_tanh)
    value = pre_value * half_up
    slope = half_up + 0.5 * pre_value * (1.0 - slope_tanh * slope_tanh) * gelu_root * (
        1.0 + 3.0 * gelu_cubic * square
    )
    return value, slope


def dot(left, right, dims=((1,), (0,))):
    return lax.dot_general(left, right, (dims, ((), ())), preferred_element_type=jnp.float32)


def slot_row(experts, slots, keep, intra_size):
    group = (experts >= intra_size).astype(jnp.int32)
    row = (experts - group * intra_size) * TILE + group * (KINDS * CAP) + slots
    return jnp.where(keep == 1, row, -TILE)


def as_column(row):
    count = row.shape[1]
    shape = (count, count)
    diagonal = lax.broadcasted_iota(jnp.int32, shape, 0) == lax.broadcasted_iota(jnp.int32, shape, 1)
    return jnp.sum(jnp.where(diagonal, row, 0.0), axis=1, keepdims=True)


def as_row(column):
    count = column.shape[0]
    shape = (count, count)
    diagonal = lax.broadcasted_iota(jnp.int32, shape, 0) == lax.broadcasted_iota(jnp.int32, shape, 1)
    return jnp.sum(jnp.where(diagonal, column, 0.0), axis=0, keepdims=True)


def place_kernel(intra_size, tokens, experts, slots, keep, gate, out_grad, send):
    count = tokens.shape[0]
    row = slot_row(experts[...], slots[...], keep[...], intra_size)
    scaled = (as_column(gate[...]) * out_grad[...].astype(jnp.float32)).astype(jnp.bfloat16)
    at = lax.broadcasted_iota(jnp.int32, (send.shape[0], count), 0)
    hot_x = (at == row).astype(jnp.bfloat16)
    hot_g = (at == row + CAP).astype(jnp.bfloat16)
    send[...] = (dot(hot_x, tokens[...]) + dot(hot_g, scaled)).astype(jnp.bfloat16)


def pick_kernel(intra_size, home, experts, slots, keep, gate, out_grad, expert_out, gate_grad, token_grad):
    count = out_grad.shape[0]
    row = slot_row(experts[...], slots[...], keep[...], intra_size)
    row = as_column(row.astype(jnp.float32)).astype(jnp.int32)
    at = lax.broadcasted_iota(jnp.int32, (count, home.shape[0]), 1)
    ffn_tok = dot((at == row).astype(jnp.bfloat16), home[...])
    expert_out[...] = (as_column(gate[...]) * ffn_tok).astype(jnp.bfloat16)
    gate_grad[...] = as_row(jnp.sum(out_grad[...].astype(jnp.float32) * ffn_tok, axis=1, keepdims=True))
    token_grad[...] = dot((at == row + CAP).astype(jnp.bfloat16), home[...]).astype(jnp.bfloat16)


def row_places(narrow, wide, first, transposed):
    half = narrow // KINDS
    shape = (wide, narrow) if transposed else (narrow, wide)
    index = lax.broadcasted_iota(jnp.int32, shape, 1 if transposed else 0)
    at = lax.broadcasted_iota(jnp.int32, shape, 0 if transposed else 1)
    kind = (index >= half).astype(jnp.int32)
    within = index - kind * half
    return (at == (within >> 1) * TILE + first + kind * CAP + (within & 1)).astype(jnp.bfloat16)


def forward_rows(group_ref, rows, weight_in, weight_out, rows_x, rows_g):
    sources, wide, _ = rows.shape
    narrow = wide // EGRP
    half = narrow // KINDS
    take = row_places(narrow, wide, group_ref[0] * (KINDS * CAP), False)
    for s in range(sources):
        taken = dot(take, rows[s]).astype(jnp.bfloat16)
        rows_x[pl.ds(s * half, half), :] = taken[:half]
        rows_g[pl.ds(s * half, half), :] = taken[half:]
    pre_act = dot(rows_x[...], weight_in[...])
    hidden_grad = dot(rows_g[...], weight_out[...], ((1,), (1,)))
    value, slope = gelu_and_slope(pre_act)
    return value.astype(jnp.bfloat16), (hidden_grad * slope).astype(jnp.bfloat16)


def expert_kernel(group_ref, rows, weight_in, weight_out, send, rows_x, rows_g):
    sources, wide, _ = rows.shape
    narrow = wide // EGRP
    half = narrow // KINDS
    hidden, pre_grad = forward_rows(group_ref, rows, weight_in, weight_out, rows_x, rows_g)
    part_out = dot(hidden, weight_out[...]).astype(jnp.bfloat16)
    part_in = dot(pre_grad, weight_in[...], ((1,), (1,))).astype(jnp.bfloat16)
    put = row_places(narrow, wide, group_ref[0] * (KINDS * CAP), True)
    for s in range(sources):
        both = jnp.concatenate([part_out[s * half : (s + 1) * half], part_in[s * half : (s + 1) * half]], axis=0)
        send[s] = dot(put, both).astype(jnp.bfloat16)


def weights_kernel(group_ref, rows, weight_in, weight_out, grad_in, grad_out, rows_x, rows_g, sum_in, sum_out):
    hidden, pre_grad = forward_rows(group_ref, rows, weight_in, weight_out, rows_x, rows_g)

    @pl.when(pl.program_id(0) == 0)
    def _():
        sum_in[...] = jnp.zeros_like(sum_in)
        sum_out[...] = jnp.zeros_like(sum_out)

    sum_in[...] += dot(rows_x[...], pre_grad, ((0,), (0,)))
    sum_out[...] += dot(hidden, rows_g[...], ((0,), (0,)))

    @pl.when(pl.program_id(0) == pl.num_programs(0) - 1)
    def _():
        grad_in[...] = sum_in[...].astype(grad_in.dtype)
        grad_out[...] = sum_out[...].astype(grad_out.dtype)


def on_device(tokens, expert_ids, slot_ids, keep_mask, gate_prob, out_grad, in_weight, out_weight):
    tok_rows, width = tokens.shape
    intra_size = lax.axis_size("intra")
    inter_size = lax.axis_size("inter")
    blocks_ff = inter_size // EGRP
    group = (lax.axis_index("inter") // blocks_ff).astype(jnp.int32).reshape(1)
    weight_in = in_weight[0, 0]
    weight_out = out_weight[0, 0]
    hidden_units = weight_in.shape[1]
    wide = intra_size * TILE
    params = pltpu.CompilerParams(vmem_limit_bytes=VMEM_BYTES)
    routing = (expert_ids[None], slot_ids[None], keep_mask[None], gate_prob[None])

    placed = pl.pallas_call(
        functools.partial(place_kernel, intra_size),
        out_shape=jax.ShapeDtypeStruct((wide, width), jnp.bfloat16),
        compiler_params=params,
        name="place",
    )(tokens, *routing, out_grad)
    moved = lax.all_to_all(placed.reshape(intra_size, TILE, width), "intra", 0, 0, tiled=True)
    spread = lax.all_gather(moved.reshape(1, wide, width), "inter", axis=0, tiled=True)

    step = 4
    rows_step = step * wide // (EGRP * KINDS)
    whole = lambda i, *_: (0, 0)
    by_plane = pl.BlockSpec((step, wide, width), lambda i, *_: (i, 0, 0))
    in_block = pl.BlockSpec((width, hidden_units), whole)
    out_block = pl.BlockSpec((hidden_units, width), whole)
    row_scratch = [pltpu.VMEM((rows_step, width), jnp.bfloat16)] * 2

    def over_planes(kernel, name, out_specs, out_shape, scratch):
        return pl.pallas_call(
            kernel,
            grid_spec=pltpu.PrefetchScalarGridSpec(
                num_scalar_prefetch=1,
                grid=(inter_size // step,),
                in_specs=[by_plane, in_block, out_block],
                out_specs=out_specs,
                scratch_shapes=row_scratch + scratch,
            ),
            out_shape=out_shape,
            compiler_params=params,
            name=name,
        )(group, spread, weight_in, weight_out)

    send = over_planes(
        expert_kernel, "expert", by_plane, jax.ShapeDtypeStruct((inter_size, wide, width), jnp.bfloat16), []
    )
    summed = lax.psum_scatter(send, "inter", scatter_dimension=0, tiled=True)
    in_weight_grad, out_weight_grad = over_planes(
        weights_kernel,
        "weight_grads",
        [in_block, out_block],
        [jax.ShapeDtypeStruct(w.shape, jnp.bfloat16) for w in (weight_in, weight_out)],
        [pltpu.VMEM(w.shape, jnp.float32) for w in (weight_in, weight_out)],
    )
    summed, out_weight_grad, in_weight_grad = lax.optimization_barrier((summed, out_weight_grad, in_weight_grad))

    home = lax.all_to_all(summed.reshape(intra_size, TILE, width), "intra", 0, 0, tiled=True)
    expert_out, gate_grad, token_grad = pl.pallas_call(
        functools.partial(pick_kernel, intra_size),
        out_shape=[
            jax.ShapeDtypeStruct((tok_rows, width), jnp.bfloat16),
            jax.ShapeDtypeStruct((1, tok_rows), jnp.float32),
            jax.ShapeDtypeStruct((tok_rows, width), jnp.bfloat16),
        ],
        compiler_params=params,
        name="pick",
    )(home.reshape(wide, width), *routing, out_grad)
    return (
        expert_out,
        gate_grad.reshape(tok_rows),
        token_grad,
        in_weight_grad[None, None],
        out_weight_grad[None, None],
    )


def solution(mesh):
    tok = P(("inter", "intra"), None)
    per = P(("inter", "intra"))
    wgt = P("inter", "intra", None, None)
    return jax.shard_map(
        on_device,
        mesh=mesh,
        in_specs=(tok, per, per, per, per, tok, wgt, wgt),
        out_specs=(tok, per, tok, wgt, wgt),
        check_vma=False,
    )
```

```python
import functools
import math

import jax
import jax.numpy as jnp
from jax import lax
from jax.experimental import pallas as pl
from jax.experimental.pallas import tpu as pltpu
from jax.sharding import PartitionSpec as P

EGRP = 2
CAP = 2
KINDS = 2
TILE = EGRP * KINDS * CAP
VMEM_BYTES = 60 * 1024 * 1024

gelu_root = math.sqrt(2.0 / math.pi)
gelu_cubic = 0.044715


def gelu_and_slope(pre_value):
    square = pre_value * pre_value
    argument = gelu_root * (pre_value + gelu_cubic * square * pre_value)
    slope_tanh = jnp.tanh(argument)
    half_up = 0.5 * (1.0 + slope_tanh)
    value = pre_value * half_up
    slope = half_up + 0.5 * pre_value * (1.0 - slope_tanh * slope_tanh) * gelu_root * (
        1.0 + 3.0 * gelu_cubic * square
    )
    return value, slope


def dot(left, right, dims=((1,), (0,))):
    return lax.dot_general(left, right, (dims, ((), ())), preferred_element_type=jnp.float32)


def slot_row(experts, slots, keep, intra_size):
    group = (experts >= intra_size).astype(jnp.int32)
    row = (experts - group * intra_size) * TILE + group * (KINDS * CAP) + slots
    return jnp.where(keep == 1, row, -TILE)


def as_column(row):
    count = row.shape[1]
    shape = (count, count)
    diagonal = lax.broadcasted_iota(jnp.int32, shape, 0) == lax.broadcasted_iota(jnp.int32, shape, 1)
    return jnp.sum(jnp.where(diagonal, row, 0.0), axis=1, keepdims=True)


def as_row(column):
    count = column.shape[0]
    shape = (count, count)
    diagonal = lax.broadcasted_iota(jnp.int32, shape, 0) == lax.broadcasted_iota(jnp.int32, shape, 1)
    return jnp.sum(jnp.where(diagonal, column, 0.0), axis=0, keepdims=True)


def place_kernel(intra_size, tokens, experts, slots, keep, gate, out_grad, send):
    count = tokens.shape[0]
    row = slot_row(experts[...], slots[...], keep[...], intra_size)
    scaled = (as_column(gate[...]) * out_grad[...].astype(jnp.float32)).astype(jnp.bfloat16)
    at = lax.broadcasted_iota(jnp.int32, (send.shape[0], count), 0)
    hot_x = (at == row).astype(jnp.bfloat16)
    hot_g = (at == row + CAP).astype(jnp.bfloat16)
    send[...] = (dot(hot_x, tokens[...]) + dot(hot_g, scaled)).astype(jnp.bfloat16)


def pick_kernel(intra_size, home, experts, slots, keep, gate, out_grad, expert_out, gate_grad, token_grad):
    count = out_grad.shape[0]
    row = slot_row(experts[...], slots[...], keep[...], intra_size)
    row = as_column(row.astype(jnp.float32)).astype(jnp.int32)
    at = lax.broadcasted_iota(jnp.int32, (count, home.shape[0]), 1)
    ffn_tok = dot((at == row).astype(jnp.bfloat16), home[...])
    expert_out[...] = (as_column(gate[...]) * ffn_tok).astype(jnp.bfloat16)
    gate_grad[...] = as_row(jnp.sum(out_grad[...].astype(jnp.float32) * ffn_tok, axis=1, keepdims=True))
    token_grad[...] = dot((at == row + CAP).astype(jnp.bfloat16), home[...]).astype(jnp.bfloat16)


def row_order(wide, transposed):
    half = wide // TILE * CAP
    shape = (wide, wide)
    index = lax.broadcasted_iota(jnp.int32, shape, 1 if transposed else 0)
    at = lax.broadcasted_iota(jnp.int32, shape, 0 if transposed else 1)
    part = sum((index >= half * k).astype(jnp.int32) for k in range(1, EGRP * KINDS))
    within = index - part * half
    return (at == (within >> 1) * TILE + part * CAP + (within & 1)).astype(jnp.bfloat16)


def order_kernel(transposed, rows, ordered):
    ordered[...] = dot(row_order(rows.shape[0], transposed), rows[...]).astype(jnp.bfloat16)


def forward_rows(rows, weight_in, weight_out):
    sources, narrow, width = rows.shape
    half = narrow // KINDS
    rows_x = rows[:, :half, :].reshape(sources * half, width)
    rows_g = rows[:, half:, :].reshape(sources * half, width)
    pre_act = dot(rows_x, weight_in[...])
    hidden_grad = dot(rows_g, weight_out[...], ((1,), (1,)))
    value, slope = gelu_and_slope(pre_act)
    return rows_x, rows_g, value.astype(jnp.bfloat16), (hidden_grad * slope).astype(jnp.bfloat16)


def expert_kernel(group_ref, rows, weight_in, weight_out, send):
    sources, narrow, width = rows.shape
    half = narrow // KINDS
    _, _, hidden, pre_grad = forward_rows(rows, weight_in, weight_out)
    part_out = dot(hidden, weight_out[...]).astype(jnp.bfloat16)
    part_in = dot(pre_grad, weight_in[...], ((1,), (1,))).astype(jnp.bfloat16)
    own = pl.multiple_of(group_ref[0] * narrow, narrow)
    other = pl.multiple_of((EGRP - 1 - group_ref[0]) * narrow, narrow)
    send[:, pl.ds(other, narrow), :] = jnp.zeros((sources, narrow, width), jnp.bfloat16)
    send[:, pl.ds(own, half), :] = part_out.reshape(sources, half, width)
    send[:, pl.ds(own + half, half), :] = part_in.reshape(sources, half, width)


def weights_kernel(group_ref, rows, weight_in, weight_out, grad_in, grad_out, sum_in, sum_out):
    rows_x, rows_g, hidden, pre_grad = forward_rows(rows, weight_in, weight_out)

    @pl.when(pl.program_id(0) == 0)
    def _():
        sum_in[...] = jnp.zeros_like(sum_in)
        sum_out[...] = jnp.zeros_like(sum_out)

    sum_in[...] += dot(rows_x, pre_grad, ((0,), (0,)))
    sum_out[...] += dot(hidden, rows_g, ((0,), (0,)))

    @pl.when(pl.program_id(0) == pl.num_programs(0) - 1)
    def _():
        grad_in[...] = sum_in[...].astype(grad_in.dtype)
        grad_out[...] = sum_out[...].astype(grad_out.dtype)


def on_device(tokens, expert_ids, slot_ids, keep_mask, gate_prob, out_grad, in_weight, out_weight):
    tok_rows, width = tokens.shape
    intra_size = lax.axis_size("intra")
    inter_size = lax.axis_size("inter")
    blocks_ff = inter_size // EGRP
    group = (lax.axis_index("inter") // blocks_ff).astype(jnp.int32).reshape(1)
    weight_in = in_weight[0, 0]
    weight_out = out_weight[0, 0]
    hidden_units = weight_in.shape[1]
    wide = intra_size * TILE
    params = pltpu.CompilerParams(vmem_limit_bytes=VMEM_BYTES)
    routing = (expert_ids[None], slot_ids[None], keep_mask[None], gate_prob[None])

    placed = pl.pallas_call(
        functools.partial(place_kernel, intra_size),
        out_shape=jax.ShapeDtypeStruct((wide, width), jnp.bfloat16),
        compiler_params=params,
        name="place",
    )(tokens, *routing, out_grad)
    moved = lax.all_to_all(placed.reshape(intra_size, TILE, width), "intra", 0, 0, tiled=True)

    def reorder(rows, transposed, name):
        return pl.pallas_call(
            functools.partial(order_kernel, transposed),
            out_shape=jax.ShapeDtypeStruct((wide, width), jnp.bfloat16),
            compiler_params=params,
            name=name,
        )(rows.reshape(wide, width))

    ordered = reorder(moved, False, "order")
    spread = lax.all_gather(ordered[None], "inter", axis=0, tiled=True)

    step = 4
    narrow = wide // EGRP
    whole = lambda i, *_: (0, 0)
    by_plane = pl.BlockSpec((step, wide, width), lambda i, *_: (i, 0, 0))
    in_block = pl.BlockSpec((width, hidden_units), whole)
    out_block = pl.BlockSpec((hidden_units, width), whole)
    own_rows = pl.BlockSpec((step, narrow, width), lambda i, group_ref: (i, group_ref[0], 0))

    def over_planes(kernel, name, out_specs, out_shape, scratch):
        return pl.pallas_call(
            kernel,
            grid_spec=pltpu.PrefetchScalarGridSpec(
                num_scalar_prefetch=1,
                grid=(inter_size // step,),
                in_specs=[own_rows, in_block, out_block],
                out_specs=out_specs,
                scratch_shapes=scratch,
            ),
            out_shape=out_shape,
            compiler_params=params,
            name=name,
        )(group, spread, weight_in, weight_out)

    send = over_planes(
        expert_kernel, "expert", by_plane, jax.ShapeDtypeStruct((inter_size, wide, width), jnp.bfloat16), []
    )
    summed = lax.psum_scatter(send, "inter", scatter_dimension=0, tiled=True)
    in_weight_grad, out_weight_grad = over_planes(
        weights_kernel,
        "weight_grads",
        [in_block, out_block],
        [jax.ShapeDtypeStruct(w.shape, jnp.bfloat16) for w in (weight_in, weight_out)],
        [pltpu.VMEM(w.shape, jnp.float32) for w in (weight_in, weight_out)],
    )
    summed, out_weight_grad, in_weight_grad = lax.optimization_barrier((summed, out_weight_grad, in_weight_grad))

    back = reorder(summed, True, "restore")
    home = lax.all_to_all(back.reshape(intra_size, TILE, width), "intra", 0, 0, tiled=True)
    expert_out, gate_grad, token_grad = pl.pallas_call(
        functools.partial(pick_kernel, intra_size),
        out_shape=[
            jax.ShapeDtypeStruct((tok_rows, width), jnp.bfloat16),
            jax.ShapeDtypeStruct((1, tok_rows), jnp.float32),
            jax.ShapeDtypeStruct((tok_rows, width), jnp.bfloat16),
        ],
        compiler_params=pltpu.CompilerParams(vmem_limit_bytes=16 * 1024 * 1024),
        name="pick",
    )(home.reshape(wide, width), *routing, out_grad)
    return (
        expert_out,
        gate_grad.reshape(tok_rows),
        token_grad,
        in_weight_grad[None, None],
        out_weight_grad[None, None],
    )


def solution(mesh):
    tok = P(("inter", "intra"), None)
    per = P(("inter", "intra"))
    wgt = P("inter", "intra", None, None)
    return jax.shard_map(
        on_device,
        mesh=mesh,
        in_specs=(tok, per, per, per, per, tok, wgt, wgt),
        out_specs=(tok, per, tok, wgt, wgt),
        check_vma=False,
    )
```

```python
import functools
import math

import jax
import jax.numpy as jnp
from jax import lax
from jax.experimental import pallas as pl
from jax.experimental.pallas import tpu as pltpu
from jax.sharding import PartitionSpec as P

EGRP = 2
CAP = 2
KINDS = 2
TILE = EGRP * KINDS * CAP
VMEM_BYTES = 60 * 1024 * 1024
VMEM_SMALL = 8 * 1024 * 1024
SMALLEST = 2.0**-126

gelu_root = math.sqrt(2.0 / math.pi)
gelu_cubic = 0.044715


def gelu_and_slope(pre_value):
    square = pre_value * pre_value
    argument = gelu_root * (pre_value + gelu_cubic * square * pre_value)
    slope_tanh = jnp.tanh(argument)
    half_up = 0.5 * (1.0 + slope_tanh)
    value = pre_value * half_up
    slope = half_up + 0.5 * pre_value * (1.0 - slope_tanh * slope_tanh) * gelu_root * (
        1.0 + 3.0 * gelu_cubic * square
    )
    return value, slope


def dot(left, right, dims=((1,), (0,))):
    return lax.dot_general(left, right, (dims, ((), ())), preferred_element_type=jnp.float32)


def slot_row(experts, slots, keep, intra_size):
    group = (experts >= intra_size).astype(jnp.int32)
    row = (experts - group * intra_size) * TILE + group * (KINDS * CAP) + slots
    return jnp.where(keep == 1, row, -TILE)


def as_column(row):
    count = row.shape[1]
    shape = (count, count)
    diagonal = lax.broadcasted_iota(jnp.int32, shape, 0) == lax.broadcasted_iota(jnp.int32, shape, 1)
    return jnp.sum(jnp.where(diagonal, row, 0.0), axis=1, keepdims=True)


def as_row(column):
    count = column.shape[0]
    shape = (count, count)
    diagonal = lax.broadcasted_iota(jnp.int32, shape, 0) == lax.broadcasted_iota(jnp.int32, shape, 1)
    return jnp.sum(jnp.where(diagonal, column, 0.0), axis=0, keepdims=True)


def place_kernel(intra_size, tokens, experts, slots, keep, gate, out_grad, send):
    count = tokens.shape[0]
    row = slot_row(experts[...], slots[...], keep[...], intra_size)
    scaled = (as_column(gate[...]) * out_grad[...].astype(jnp.float32)).astype(jnp.bfloat16)
    at = lax.broadcasted_iota(jnp.int32, (send.shape[0], count), 0)
    hot_x = (at == row).astype(jnp.bfloat16)
    hot_g = (at == row + CAP).astype(jnp.bfloat16)
    send[...] = (dot(hot_x, tokens[...]) + dot(hot_g, scaled)).astype(jnp.bfloat16)


def pick_kernel(intra_size, home, experts, slots, keep, gate, out_grad, expert_out, gate_grad, token_grad):
    count = out_grad.shape[0]
    row = slot_row(experts[...], slots[...], keep[...], intra_size)
    row = as_column(row.astype(jnp.float32)).astype(jnp.int32)
    at = lax.broadcasted_iota(jnp.int32, (count, home.shape[0]), 1)
    ffn_tok = dot((at == row).astype(jnp.bfloat16), home[...])
    expert_out[...] = (as_column(gate[...]) * ffn_tok).astype(jnp.bfloat16)
    gate_grad[...] = as_row(jnp.sum(out_grad[...].astype(jnp.float32) * ffn_tok, axis=1, keepdims=True))
    token_grad[...] = dot((at == row + CAP).astype(jnp.bfloat16), home[...]).astype(jnp.bfloat16)


def row_order(wide, transposed):
    half = wide // TILE * CAP
    shape = (wide, wide)
    index = lax.broadcasted_iota(jnp.int32, shape, 1 if transposed else 0)
    at = lax.broadcasted_iota(jnp.int32, shape, 0 if transposed else 1)
    part = sum((index >= half * k).astype(jnp.int32) for k in range(1, EGRP * KINDS))
    within = index - part * half
    return (at == (within >> 1) * TILE + part * CAP + (within & 1)).astype(jnp.bfloat16)


def encode(value):
    size = jnp.maximum(jnp.abs(value), SMALLEST)
    exponent = jnp.floor(jnp.log2(size))
    code = jnp.round((exponent + 126.0) * 128.0 + size * jnp.exp2(-exponent) * 128.0)
    code = jnp.where(jnp.abs(value) < SMALLEST, 0.0, code)
    return jnp.where(value < 0.0, -code, code).astype(jnp.int32).astype(jnp.int16)


def decode(code):
    wide = code.astype(jnp.int32)
    size = jnp.abs(wide)
    mantissa = ((size & 127) + 128).astype(jnp.float32) * (1.0 / 128.0)
    value = mantissa * jnp.exp2((size >> 7).astype(jnp.float32) - 127.0)
    value = jnp.where(size < 128, 0.0, value)
    return jnp.where(wide < 0, -value, value).astype(jnp.bfloat16)


def order_kernel(transposed, rows, ordered):
    moved = dot(row_order(rows.shape[0], transposed), rows[...])
    ordered[...] = moved.astype(jnp.bfloat16) if transposed else encode(moved)


def forward_rows(rows, weight_in, weight_out):
    sources, narrow, width = rows.shape
    half = narrow // KINDS
    rows_x = decode(rows[:, :half, :]).reshape(sources * half, width)
    rows_g = decode(rows[:, half:, :]).reshape(sources * half, width)
    pre_act = dot(rows_x, weight_in[...])
    hidden_grad = dot(rows_g, weight_out[...], ((1,), (1,)))
    value, slope = gelu_and_slope(pre_act)
    return rows_x, rows_g, value.astype(jnp.bfloat16), (hidden_grad * slope).astype(jnp.bfloat16)


def expert_kernel(group_ref, rows, weight_in, weight_out, send):
    sources, narrow, width = rows.shape
    half = narrow // KINDS
    _, _, hidden, pre_grad = forward_rows(rows, weight_in, weight_out)
    part_out = dot(hidden, weight_out[...]).astype(jnp.bfloat16)
    part_in = dot(pre_grad, weight_in[...], ((1,), (1,))).astype(jnp.bfloat16)
    own = pl.multiple_of(group_ref[0] * narrow, narrow)
    other = pl.multiple_of((EGRP - 1 - group_ref[0]) * narrow, narrow)
    send[:, pl.ds(other, narrow), :] = jnp.zeros((sources, narrow, width), jnp.bfloat16)
    send[:, pl.ds(own, half), :] = part_out.reshape(sources, half, width)
    send[:, pl.ds(own + half, half), :] = part_in.reshape(sources, half, width)


def weights_kernel(group_ref, rows, weight_in, weight_out, grad_in, grad_out, sum_in, sum_out):
    rows_x, rows_g, hidden, pre_grad = forward_rows(rows, weight_in, weight_out)

    @pl.when(pl.program_id(0) == 0)
    def _():
        sum_in[...] = jnp.zeros_like(sum_in)
        sum_out[...] = jnp.zeros_like(sum_out)

    sum_in[...] += dot(rows_x, pre_grad, ((0,), (0,)))
    sum_out[...] += dot(hidden, rows_g, ((0,), (0,)))

    @pl.when(pl.program_id(0) == pl.num_programs(0) - 1)
    def _():
        grad_in[...] = sum_in[...].astype(grad_in.dtype)
        grad_out[...] = sum_out[...].astype(grad_out.dtype)


def on_device(tokens, expert_ids, slot_ids, keep_mask, gate_prob, out_grad, in_weight, out_weight):
    tok_rows, width = tokens.shape
    intra_size = lax.axis_size("intra")
    inter_size = lax.axis_size("inter")
    blocks_ff = inter_size // EGRP
    group = (lax.axis_index("inter") // blocks_ff).astype(jnp.int32).reshape(1)
    weight_in = in_weight[0, 0]
    weight_out = out_weight[0, 0]
    hidden_units = weight_in.shape[1]
    wide = intra_size * TILE
    params = pltpu.CompilerParams(vmem_limit_bytes=VMEM_BYTES)
    routing = (expert_ids[None], slot_ids[None], keep_mask[None], gate_prob[None])

    placed = pl.pallas_call(
        functools.partial(place_kernel, intra_size),
        out_shape=jax.ShapeDtypeStruct((wide, width), jnp.bfloat16),
        compiler_params=params,
        name="place",
    )(tokens, *routing, out_grad)
    moved = lax.all_to_all(placed.reshape(intra_size, TILE, width), "intra", 0, 0, tiled=True)

    def reorder(rows, transposed, name):
        return pl.pallas_call(
            functools.partial(order_kernel, transposed),
            out_shape=jax.ShapeDtypeStruct((wide, width), jnp.bfloat16 if transposed else jnp.int16),
            compiler_params=pltpu.CompilerParams(vmem_limit_bytes=VMEM_SMALL),
            name=name,
        )(rows.reshape(wide, width))

    ordered = reorder(moved, False, "order")
    spread = lax.all_gather(ordered[None], "inter", axis=0, tiled=True)

    step = 4
    narrow = wide // EGRP
    whole = lambda i, *_: (0, 0)
    by_plane = pl.BlockSpec((step, wide, width), lambda i, *_: (i, 0, 0))
    in_block = pl.BlockSpec((width, hidden_units), whole)
    out_block = pl.BlockSpec((hidden_units, width), whole)
    own_rows = pl.BlockSpec((step, narrow, width), lambda i, group_ref: (i, group_ref[0], 0))

    def over_planes(kernel, name, out_specs, out_shape, scratch):
        return pl.pallas_call(
            kernel,
            grid_spec=pltpu.PrefetchScalarGridSpec(
                num_scalar_prefetch=1,
                grid=(inter_size // step,),
                in_specs=[own_rows, in_block, out_block],
                out_specs=out_specs,
                scratch_shapes=scratch,
            ),
            out_shape=out_shape,
            compiler_params=params,
            name=name,
        )(group, spread, weight_in, weight_out)

    send = over_planes(
        expert_kernel, "expert", by_plane, jax.ShapeDtypeStruct((inter_size, wide, width), jnp.bfloat16), []
    )
    summed = lax.psum_scatter(send, "inter", scatter_dimension=0, tiled=True)
    in_weight_grad, out_weight_grad = over_planes(
        weights_kernel,
        "weight_grads",
        [in_block, out_block],
        [jax.ShapeDtypeStruct(w.shape, jnp.bfloat16) for w in (weight_in, weight_out)],
        [pltpu.VMEM(w.shape, jnp.float32) for w in (weight_in, weight_out)],
    )
    summed, out_weight_grad, in_weight_grad = lax.optimization_barrier((summed, out_weight_grad, in_weight_grad))

    back = reorder(summed, True, "restore")
    home = lax.all_to_all(back.reshape(intra_size, TILE, width), "intra", 0, 0, tiled=True)
    expert_out, gate_grad, token_grad = pl.pallas_call(
        functools.partial(pick_kernel, intra_size),
        out_shape=[
            jax.ShapeDtypeStruct((tok_rows, width), jnp.bfloat16),
            jax.ShapeDtypeStruct((1, tok_rows), jnp.float32),
            jax.ShapeDtypeStruct((tok_rows, width), jnp.bfloat16),
        ],
        compiler_params=pltpu.CompilerParams(vmem_limit_bytes=VMEM_SMALL),
        name="pick",
    )(home.reshape(wide, width), *routing, out_grad)
    return (
        expert_out,
        gate_grad.reshape(tok_rows),
        token_grad,
        in_weight_grad[None, None],
        out_weight_grad[None, None],
    )


def solution(mesh):
    tok = P(("inter", "intra"), None)
    per = P(("inter", "intra"))
    wgt = P("inter", "intra", None, None)
    return jax.shard_map(
        on_device,
        mesh=mesh,
        in_specs=(tok, per, per, per, per, tok, wgt, wgt),
        out_specs=(tok, per, tok, wgt, wgt),
        check_vma=False,
    )
```

```python
import functools
import math

import jax
import jax.numpy as jnp
from jax import lax
from jax.experimental import pallas as pl
from jax.experimental.pallas import tpu as pltpu
from jax.sharding import PartitionSpec as P

EGRP = 2
CAP = 2
KINDS = 2
TILE = KINDS * CAP
VMEM_BYTES = 60 * 1024 * 1024
VMEM_SMALL = 8 * 1024 * 1024
STEPS = 229.0
OCTAVES = 140.0
SMALLEST = 2.0**-126

gelu_root = math.sqrt(2.0 / math.pi)
gelu_cubic = 0.044715


def gelu_and_slope(pre_value):
    square = pre_value * pre_value
    argument = gelu_root * (pre_value + gelu_cubic * square * pre_value)
    slope_tanh = jnp.tanh(argument)
    half_up = 0.5 * (1.0 + slope_tanh)
    value = pre_value * half_up
    slope = half_up + 0.5 * pre_value * (1.0 - slope_tanh * slope_tanh) * gelu_root * (
        1.0 + 3.0 * gelu_cubic * square
    )
    return value, slope


def dot(left, right, dims=((1,), (0,))):
    return lax.dot_general(left, right, (dims, ((), ())), preferred_element_type=jnp.float32)


def encode(value):
    size = jnp.abs(value)
    code = jnp.round((jnp.log2(jnp.maximum(size, SMALLEST)) + OCTAVES) * STEPS)
    code = jnp.where(size < SMALLEST, 0.0, code)
    return jnp.where(value < 0.0, -code, code).astype(jnp.int32).astype(jnp.int16)


def decode(code):
    wide = code.astype(jnp.int32).astype(jnp.float32)
    value = jnp.exp2(jnp.abs(wide) * (1.0 / STEPS) - OCTAVES)
    return jnp.where(wide < 0.0, -value, value).astype(jnp.bfloat16)


def as_column(row):
    count = row.shape[1]
    shape = (count, count)
    diagonal = lax.broadcasted_iota(jnp.int32, shape, 0) == lax.broadcasted_iota(jnp.int32, shape, 1)
    return jnp.sum(jnp.where(diagonal, row, 0.0), axis=1, keepdims=True)


def as_row(column):
    count = column.shape[0]
    shape = (count, count)
    diagonal = lax.broadcasted_iota(jnp.int32, shape, 0) == lax.broadcasted_iota(jnp.int32, shape, 1)
    return jnp.sum(jnp.where(diagonal, column, 0.0), axis=0, keepdims=True)


def slot_row(experts, slots, keep):
    return jnp.where(keep == 1, experts * TILE + slots, -TILE)


def place_kernel(tokens, experts, slots, keep, gate, out_grad, send):
    count = tokens.shape[0]
    row = slot_row(experts[...], slots[...], keep[...])
    scaled = (as_column(gate[...]) * out_grad[...].astype(jnp.float32)).astype(jnp.bfloat16)
    at = lax.broadcasted_iota(jnp.int32, (send.shape[0], count), 0)
    hot_x = (at == row).astype(jnp.bfloat16)
    hot_g = (at == row + CAP).astype(jnp.bfloat16)
    send[...] = (dot(hot_x, tokens[...]) + dot(hot_g, scaled)).astype(jnp.bfloat16)


def pick_kernel(home, experts, slots, keep, gate, out_grad, expert_out, gate_grad, token_grad):
    count = out_grad.shape[0]
    row = slot_row(experts[...], slots[...], keep[...])
    row = as_column(row.astype(jnp.float32)).astype(jnp.int32)
    at = lax.broadcasted_iota(jnp.int32, (count, home.shape[0]), 1)
    ffn_tok = dot((at == row).astype(jnp.bfloat16), home[...])
    expert_out[...] = (as_column(gate[...]) * ffn_tok).astype(jnp.bfloat16)
    gate_grad[...] = as_row(jnp.sum(out_grad[...].astype(jnp.float32) * ffn_tok, axis=1, keepdims=True))
    token_grad[...] = dot((at == row + CAP).astype(jnp.bfloat16), home[...]).astype(jnp.bfloat16)


def row_order(wide, transposed):
    half = wide // KINDS
    shape = (wide, wide)
    index = lax.broadcasted_iota(jnp.int32, shape, 1 if transposed else 0)
    at = lax.broadcasted_iota(jnp.int32, shape, 0 if transposed else 1)
    kind = (index >= half).astype(jnp.int32)
    within = index - half * kind
    return (at == (within >> 1) * TILE + kind * CAP + (within & 1)).astype(jnp.bfloat16)


def order_kernel(transposed, rows, ordered):
    moved = dot(row_order(rows.shape[0], transposed), rows[...])
    ordered[...] = moved.astype(jnp.bfloat16) if transposed else encode(moved)


def forward_rows(rows, weight_in, weight_out):
    sources, wide, width = rows.shape
    half = wide // KINDS
    rows_x = decode(rows[:, :half, :]).reshape(sources * half, width)
    rows_g = decode(rows[:, half:, :]).reshape(sources * half, width)
    pre_act = dot(rows_x, weight_in[...])
    hidden_grad = dot(rows_g, weight_out[...], ((1,), (1,)))
    value, slope = gelu_and_slope(pre_act)
    return rows_x, rows_g, value.astype(jnp.bfloat16), (hidden_grad * slope).astype(jnp.bfloat16)


def expert_kernel(rows, weight_in, weight_out, send):
    sources, wide, width = rows.shape
    half = wide // KINDS
    _, _, hidden, pre_grad = forward_rows(rows, weight_in, weight_out)
    part_out = dot(hidden, weight_out[...]).astype(jnp.bfloat16)
    part_in = dot(pre_grad, weight_in[...], ((1,), (1,))).astype(jnp.bfloat16)
    send[:, :half, :] = part_out.reshape(sources, half, width)
    send[:, half:, :] = part_in.reshape(sources, half, width)


def weights_kernel(rows, weight_in, weight_out, grad_in, grad_out, sum_in, sum_out):
    rows_x, rows_g, hidden, pre_grad = forward_rows(rows, weight_in, weight_out)

    @pl.when(pl.program_id(0) == 0)
    def _():
        sum_in[...] = jnp.zeros_like(sum_in)
        sum_out[...] = jnp.zeros_like(sum_out)

    sum_in[...] += dot(rows_x, pre_grad, ((0,), (0,)))
    sum_out[...] += dot(hidden, rows_g, ((0,), (0,)))

    @pl.when(pl.program_id(0) == pl.num_programs(0) - 1)
    def _():
        grad_in[...] = sum_in[...].astype(grad_in.dtype)
        grad_out[...] = sum_out[...].astype(grad_out.dtype)


def partner_groups(inter_size, intra_size):
    return [
        [plane * intra_size + index for plane in (low, inter_size - 1 - low) for index in range(intra_size)]
        for low in range(inter_size // EGRP)
    ]


def group_order(inter_size):
    blocks = inter_size // EGRP
    low = list(range(0, blocks, 2)) + list(range(blocks - 1 - blocks % 2, 0, -2))
    return [low, [inter_size - 1 - plane for plane in low]]


def on_device(tokens, expert_ids, slot_ids, keep_mask, gate_prob, out_grad, in_weight, out_weight):
    tok_rows, width = tokens.shape
    intra_size = lax.axis_size("intra")
    inter_size = lax.axis_size("inter")
    blocks_ff = inter_size // EGRP
    partners = EGRP * intra_size
    weight_in = in_weight[0, 0]
    weight_out = out_weight[0, 0]
    hidden_units = weight_in.shape[1]
    wide = partners * TILE
    params = pltpu.CompilerParams(vmem_limit_bytes=VMEM_BYTES)
    small = pltpu.CompilerParams(vmem_limit_bytes=VMEM_SMALL)
    routing = (expert_ids[None], slot_ids[None], keep_mask[None], gate_prob[None])
    groups = group_order(inter_size)

    def exchange(rows):
        moved = lax.all_to_all(
            rows.reshape(partners, TILE, width),
            ("inter", "intra"),
            0,
            0,
            axis_index_groups=partner_groups(inter_size, intra_size),
            tiled=True,
        )
        return moved.reshape(wide, width)

    def reorder(rows, transposed, name):
        return pl.pallas_call(
            functools.partial(order_kernel, transposed),
            out_shape=jax.ShapeDtypeStruct((wide, width), jnp.bfloat16 if transposed else jnp.int16),
            compiler_params=small,
            name=name,
        )(rows)

    placed = pl.pallas_call(
        place_kernel,
        out_shape=jax.ShapeDtypeStruct((wide, width), jnp.bfloat16),
        compiler_params=params,
        name="place",
    )(tokens, *routing, out_grad)
    ordered = reorder(exchange(placed), False, "order")
    spread = lax.all_gather(ordered, "inter", axis=0, axis_index_groups=groups, tiled=True)
    spread = spread.reshape(blocks_ff, wide, width)

    step = 2
    whole = lambda i: (0, 0)
    by_plane = pl.BlockSpec((step, wide, width), lambda i: (i, 0, 0))
    in_block = pl.BlockSpec((width, hidden_units), whole)
    out_block = pl.BlockSpec((hidden_units, width), whole)

    def over_planes(kernel, name, out_specs, out_shape, scratch):
        return pl.pallas_call(
            kernel,
            grid=(blocks_ff // step,),
            in_specs=[by_plane, in_block, out_block],
            out_specs=out_specs,
            scratch_shapes=scratch,
            out_shape=out_shape,
            compiler_params=params,
            name=name,
        )(spread, weight_in, weight_out)

    send = over_planes(
        expert_kernel, "expert", by_plane, jax.ShapeDtypeStruct((blocks_ff, wide, width), jnp.bfloat16), []
    )
    summed = lax.psum_scatter(
        send.reshape(blocks_ff * wide, width), "inter", scatter_dimension=0, axis_index_groups=groups, tiled=True
    )
    in_weight_grad, out_weight_grad = over_planes(
        weights_kernel,
        "weight_grads",
        [in_block, out_block],
        [jax.ShapeDtypeStruct(w.shape, jnp.bfloat16) for w in (weight_in, weight_out)],
        [pltpu.VMEM(w.shape, jnp.float32) for w in (weight_in, weight_out)],
    )
    summed, out_weight_grad, in_weight_grad = lax.optimization_barrier((summed, out_weight_grad, in_weight_grad))

    home = exchange(reorder(summed, True, "restore"))
    expert_out, gate_grad, token_grad = pl.pallas_call(
        pick_kernel,
        out_shape=[
            jax.ShapeDtypeStruct((tok_rows, width), jnp.bfloat16),
            jax.ShapeDtypeStruct((1, tok_rows), jnp.float32),
            jax.ShapeDtypeStruct((tok_rows, width), jnp.bfloat16),
        ],
        compiler_params=small,
        name="pick",
    )(home, *routing, out_grad)
    return (
        expert_out,
        gate_grad.reshape(tok_rows),
        token_grad,
        in_weight_grad[None, None],
        out_weight_grad[None, None],
    )


def solution(mesh):
    tok = P(("inter", "intra"), None)
    per = P(("inter", "intra"))
    wgt = P("inter", "intra", None, None)
    return jax.shard_map(
        on_device,
        mesh=mesh,
        in_specs=(tok, per, per, per, per, tok, wgt, wgt),
        out_specs=(tok, per, tok, wgt, wgt),
        check_vma=False,
    )
```

```python
import functools
import math

import jax
import jax.numpy as jnp
from jax import lax
from jax.experimental import pallas as pl
from jax.experimental.pallas import tpu as pltpu
from jax.sharding import PartitionSpec as P

EGRP = 2
CAP = 2
KINDS = 2
TILE = EGRP * KINDS * CAP
VMEM_BYTES = 60 * 1024 * 1024
VMEM_SMALL = 8 * 1024 * 1024
STEPS = 229.0
OCTAVES = 140.0
SMALLEST = 2.0**-126

gelu_root = math.sqrt(2.0 / math.pi)
gelu_cubic = 0.044715


def gelu_and_slope(pre_value):
    square = pre_value * pre_value
    argument = gelu_root * (pre_value + gelu_cubic * square * pre_value)
    slope_tanh = jnp.tanh(argument)
    half_up = 0.5 * (1.0 + slope_tanh)
    value = pre_value * half_up
    slope = half_up + 0.5 * pre_value * (1.0 - slope_tanh * slope_tanh) * gelu_root * (
        1.0 + 3.0 * gelu_cubic * square
    )
    return value, slope


def dot(left, right, dims=((1,), (0,))):
    return lax.dot_general(left, right, (dims, ((), ())), preferred_element_type=jnp.float32)


def slot_row(experts, slots, keep, intra_size):
    group = (experts >= intra_size).astype(jnp.int32)
    row = (experts - group * intra_size) * TILE + group * (KINDS * CAP) + slots
    return jnp.where(keep == 1, row, -TILE)


def as_column(row):
    count = row.shape[1]
    shape = (count, count)
    diagonal = lax.broadcasted_iota(jnp.int32, shape, 0) == lax.broadcasted_iota(jnp.int32, shape, 1)
    return jnp.sum(jnp.where(diagonal, row, 0.0), axis=1, keepdims=True)


def as_row(column):
    count = column.shape[0]
    shape = (count, count)
    diagonal = lax.broadcasted_iota(jnp.int32, shape, 0) == lax.broadcasted_iota(jnp.int32, shape, 1)
    return jnp.sum(jnp.where(diagonal, column, 0.0), axis=0, keepdims=True)


def place_kernel(intra_size, tokens, experts, slots, keep, gate, out_grad, send):
    count = tokens.shape[0]
    row = slot_row(experts[...], slots[...], keep[...], intra_size)
    scaled = (as_column(gate[...]) * out_grad[...].astype(jnp.float32)).astype(jnp.bfloat16)
    at = lax.broadcasted_iota(jnp.int32, (send.shape[0], count), 0)
    hot_x = (at == row).astype(jnp.bfloat16)
    hot_g = (at == row + CAP).astype(jnp.bfloat16)
    send[...] = (dot(hot_x, tokens[...]) + dot(hot_g, scaled)).astype(jnp.bfloat16)


def pick_kernel(intra_size, home, experts, slots, keep, gate, out_grad, expert_out, gate_grad, token_grad):
    count = out_grad.shape[0]
    row = slot_row(experts[...], slots[...], keep[...], intra_size)
    row = as_column(row.astype(jnp.float32)).astype(jnp.int32)
    at = lax.broadcasted_iota(jnp.int32, (count, home.shape[0]), 1)
    ffn_tok = dot((at == row).astype(jnp.bfloat16), home[...])
    expert_out[...] = (as_column(gate[...]) * ffn_tok).astype(jnp.bfloat16)
    gate_grad[...] = as_row(jnp.sum(out_grad[...].astype(jnp.float32) * ffn_tok, axis=1, keepdims=True))
    token_grad[...] = dot((at == row + CAP).astype(jnp.bfloat16), home[...]).astype(jnp.bfloat16)


def row_order(wide, kind_first, transposed):
    part_rows = wide // TILE * CAP
    shape = (wide, wide)
    index = lax.broadcasted_iota(jnp.int32, shape, 1 if transposed else 0)
    at = lax.broadcasted_iota(jnp.int32, shape, 0 if transposed else 1)
    part = sum((index >= part_rows * k).astype(jnp.int32) for k in range(1, EGRP * KINDS))
    within = index - part * part_rows
    if kind_first:
        part = (part & 1) * KINDS + (part >> 1)
    return (at == (within >> 1) * TILE + part * CAP + (within & 1)).astype(jnp.bfloat16)


def encode(value):
    size = jnp.abs(value)
    code = jnp.round((jnp.log2(jnp.maximum(size, SMALLEST)) + OCTAVES) * STEPS)
    code = jnp.where(size < SMALLEST, 0.0, code)
    return jnp.where(value < 0.0, -code, code).astype(jnp.int32).astype(jnp.int16)


def decode(code):
    wide = code.astype(jnp.int32).astype(jnp.float32)
    value = jnp.exp2(jnp.abs(wide) * (1.0 / STEPS) - OCTAVES)
    return jnp.where(wide < 0.0, -value, value).astype(jnp.bfloat16)


def order_kernel(rows, codes_x, rows_g):
    moved = dot(row_order(rows.shape[0], True, False), rows[...])
    half = rows.shape[0] // KINDS
    codes_x[...] = encode(moved[:half])
    rows_g[...] = moved[half:].astype(jnp.bfloat16)


def restore_kernel(rows, restored):
    restored[...] = dot(row_order(rows.shape[0], False, True), rows[...]).astype(jnp.bfloat16)


def flat(rows):
    sources, count, width = rows.shape
    return rows.reshape(sources * count, width)


def activation_kernel(group_ref, codes_x, weight_in, weight_out, send, slopes):
    sources, part, width = codes_x.shape
    value, slope = gelu_and_slope(dot(flat(decode(codes_x[...])), weight_in[...]))
    slopes[...] = slope
    part_out = dot(value.astype(jnp.bfloat16), weight_out[...]).astype(jnp.bfloat16)
    own = pl.multiple_of(group_ref[0] * (KINDS * part), part)
    send[...] = jnp.zeros(send.shape, jnp.bfloat16)
    send[:, pl.ds(own, part), :] = part_out.reshape(sources, part, width)


def gradient_kernel(group_ref, rows_g, slopes, weight_in, weight_out, begun, send):
    hidden_grad = dot(flat(rows_g[...]), weight_out[...], ((1,), (1,)))
    pre_grad = (hidden_grad * slopes[...]).astype(jnp.bfloat16)
    send[...] = dot(pre_grad, weight_in[...], ((1,), (1,))).astype(jnp.bfloat16).reshape(send.shape)


def weights_kernel(group_ref, codes_x, rows_g, weight_in, weight_out, grad_in, grad_out, sum_in, sum_out):
    x = flat(decode(codes_x[...]))
    g = flat(rows_g[...])
    value, slope = gelu_and_slope(dot(x, weight_in[...]))
    hidden = value.astype(jnp.bfloat16)
    pre_grad = (dot(g, weight_out[...], ((1,), (1,))) * slope).astype(jnp.bfloat16)

    @pl.when(pl.program_id(0) == 0)
    def _():
        sum_in[...] = jnp.zeros_like(sum_in)
        sum_out[...] = jnp.zeros_like(sum_out)

    sum_in[...] += dot(x, pre_grad, ((0,), (0,)))
    sum_out[...] += dot(hidden, g, ((0,), (0,)))

    @pl.when(pl.program_id(0) == pl.num_programs(0) - 1)
    def _():
        grad_in[...] = sum_in[...].astype(grad_in.dtype)
        grad_out[...] = sum_out[...].astype(grad_out.dtype)


def on_device(tokens, expert_ids, slot_ids, keep_mask, gate_prob, out_grad, in_weight, out_weight):
    tok_rows, width = tokens.shape
    intra_size = lax.axis_size("intra")
    inter_size = lax.axis_size("inter")
    blocks_ff = inter_size // EGRP
    group = (lax.axis_index("inter") // blocks_ff).astype(jnp.int32).reshape(1)
    weight_in = in_weight[0, 0]
    weight_out = out_weight[0, 0]
    hidden_units = weight_in.shape[1]
    wide = intra_size * TILE
    params = pltpu.CompilerParams(vmem_limit_bytes=VMEM_BYTES)
    small = pltpu.CompilerParams(vmem_limit_bytes=VMEM_SMALL)
    routing = (expert_ids[None], slot_ids[None], keep_mask[None], gate_prob[None])

    placed = pl.pallas_call(
        functools.partial(place_kernel, intra_size),
        out_shape=jax.ShapeDtypeStruct((wide, width), jnp.bfloat16),
        compiler_params=params,
        name="place",
    )(tokens, *routing, out_grad)
    moved = lax.all_to_all(placed.reshape(intra_size, TILE, width), "intra", 0, 0, tiled=True)
    part = wide // (EGRP * KINDS)
    ordered_x, ordered_g = pl.pallas_call(
        order_kernel,
        out_shape=[
            jax.ShapeDtypeStruct((EGRP * part, width), jnp.int16),
            jax.ShapeDtypeStruct((EGRP * part, width), jnp.bfloat16),
        ],
        compiler_params=small,
        name="order",
    )(moved.reshape(wide, width))
    spread_g = lax.all_gather(ordered_g[None], "inter", axis=0, tiled=True)
    spread_x = lax.all_gather(ordered_x[None], "inter", axis=0, tiled=True)

    step = 4
    rows_all = inter_size * part
    whole = lambda i, group_ref: (0, 0)
    by_plane = pl.BlockSpec((step, wide, width), lambda i, group_ref: (i, 0, 0))
    own_rows = pl.BlockSpec((step, part, width), lambda i, group_ref: (i, group_ref[0], 0))
    own_gradients = pl.BlockSpec((step, part, width), lambda i, group_ref: (i, group_ref[0] * KINDS + 1, 0))
    by_row = pl.BlockSpec((step * part, hidden_units), lambda i, group_ref: (i, 0))
    in_block = pl.BlockSpec((width, hidden_units), whole)
    out_block = pl.BlockSpec((hidden_units, width), whole)
    send_shape = jax.ShapeDtypeStruct((inter_size, wide, width), jnp.bfloat16)

    def over_planes(kernel, name, in_specs, out_specs, out_shape, operands, scratch=(), aliases={}):
        return pl.pallas_call(
            kernel,
            grid_spec=pltpu.PrefetchScalarGridSpec(
                num_scalar_prefetch=1,
                grid=(inter_size // step,),
                in_specs=in_specs,
                out_specs=out_specs,
                scratch_shapes=scratch,
            ),
            out_shape=out_shape,
            input_output_aliases=aliases,
            compiler_params=params,
            name=name,
        )(group, *operands)

    begun, slopes = over_planes(
        activation_kernel,
        "activations",
        [own_rows, in_block, out_block],
        [by_plane, by_row],
        [send_shape, jax.ShapeDtypeStruct((rows_all, hidden_units), jnp.float32)],
        (spread_x, weight_in, weight_out),
    )
    send = over_planes(
        gradient_kernel,
        "gradients",
        [own_rows, by_row, in_block, out_block, pl.BlockSpec(memory_space=pl.ANY)],
        own_gradients,
        send_shape,
        (spread_g, slopes, weight_in, weight_out, begun),
        aliases={5: 0},
    )
    summed = lax.psum_scatter(send, "inter", scatter_dimension=0, tiled=True)
    in_weight_grad, out_weight_grad = over_planes(
        weights_kernel,
        "weight_grads",
        [own_rows, own_rows, in_block, out_block],
        [in_block, out_block],
        [jax.ShapeDtypeStruct(w.shape, jnp.bfloat16) for w in (weight_in, weight_out)],
        (spread_x, spread_g, weight_in, weight_out),
        scratch=[pltpu.VMEM(w.shape, jnp.float32) for w in (weight_in, weight_out)],
    )
    summed, out_weight_grad, in_weight_grad = lax.optimization_barrier((summed, out_weight_grad, in_weight_grad))

    back = pl.pallas_call(
        restore_kernel,
        out_shape=jax.ShapeDtypeStruct((wide, width), jnp.bfloat16),
        compiler_params=small,
        name="restore",
    )(summed.reshape(wide, width))
    home = lax.all_to_all(back.reshape(intra_size, TILE, width), "intra", 0, 0, tiled=True)
    expert_out, gate_grad, token_grad = pl.pallas_call(
        functools.partial(pick_kernel, intra_size),
        out_shape=[
            jax.ShapeDtypeStruct((tok_rows, width), jnp.bfloat16),
            jax.ShapeDtypeStruct((1, tok_rows), jnp.float32),
            jax.ShapeDtypeStruct((tok_rows, width), jnp.bfloat16),
        ],
        compiler_params=small,
        name="pick",
    )(home.reshape(wide, width), *routing, out_grad)
    return (
        expert_out,
        gate_grad.reshape(tok_rows),
        token_grad,
        in_weight_grad[None, None],
        out_weight_grad[None, None],
    )


def solution(mesh):
    tok = P(("inter", "intra"), None)
    per = P(("inter", "intra"))
    wgt = P("inter", "intra", None, None)
    return jax.shard_map(
        on_device,
        mesh=mesh,
        in_specs=(tok, per, per, per, per, tok, wgt, wgt),
        out_specs=(tok, per, tok, wgt, wgt),
        check_vma=False,
    )
```

```python
import functools
import math

import jax
import jax.numpy as jnp
from jax import lax
from jax.experimental import pallas as pl
from jax.experimental.pallas import tpu as pltpu
from jax.sharding import PartitionSpec as P

EGRP = 2
CAP = 2
KINDS = 2
TILE = EGRP * KINDS * CAP
VMEM_BYTES = 60 * 1024 * 1024
VMEM_SMALL = 8 * 1024 * 1024
STEPS = 229.0
OCTAVES = 140.0
SMALLEST = 2.0**-126

gelu_root = math.sqrt(2.0 / math.pi)
gelu_cubic = 0.044715


def gelu_and_slope(pre_value):
    square = pre_value * pre_value
    argument = gelu_root * (pre_value + gelu_cubic * square * pre_value)
    slope_tanh = jnp.tanh(argument)
    half_up = 0.5 * (1.0 + slope_tanh)
    value = pre_value * half_up
    slope = half_up + 0.5 * pre_value * (1.0 - slope_tanh * slope_tanh) * gelu_root * (
        1.0 + 3.0 * gelu_cubic * square
    )
    return value, slope


def dot(left, right, dims=((1,), (0,))):
    return lax.dot_general(left, right, (dims, ((), ())), preferred_element_type=jnp.float32)


def slot_row(experts, slots, keep, intra_size):
    group = (experts >= intra_size).astype(jnp.int32)
    row = (experts - group * intra_size) * TILE + group * (KINDS * CAP) + slots
    return jnp.where(keep == 1, row, -TILE)


def as_column(row):
    count = row.shape[1]
    shape = (count, count)
    diagonal = lax.broadcasted_iota(jnp.int32, shape, 0) == lax.broadcasted_iota(jnp.int32, shape, 1)
    return jnp.sum(jnp.where(diagonal, row, 0.0), axis=1, keepdims=True)


def as_row(column):
    count = column.shape[0]
    shape = (count, count)
    diagonal = lax.broadcasted_iota(jnp.int32, shape, 0) == lax.broadcasted_iota(jnp.int32, shape, 1)
    return jnp.sum(jnp.where(diagonal, column, 0.0), axis=0, keepdims=True)


def place_kernel(intra_size, tokens, experts, slots, keep, gate, out_grad, send):
    count = tokens.shape[0]
    row = slot_row(experts[...], slots[...], keep[...], intra_size)
    scaled = (as_column(gate[...]) * out_grad[...].astype(jnp.float32)).astype(jnp.bfloat16)
    at = lax.broadcasted_iota(jnp.int32, (send.shape[0], count), 0)
    hot_x = (at == row).astype(jnp.bfloat16)
    hot_g = (at == row + CAP).astype(jnp.bfloat16)
    send[...] = (dot(hot_x, tokens[...]) + dot(hot_g, scaled)).astype(jnp.bfloat16)


def pick_kernel(intra_size, home, experts, slots, keep, gate, out_grad, expert_out, gate_grad, token_grad):
    count = out_grad.shape[0]
    row = slot_row(experts[...], slots[...], keep[...], intra_size)
    row = as_column(row.astype(jnp.float32)).astype(jnp.int32)
    at = lax.broadcasted_iota(jnp.int32, (count, home.shape[0]), 1)
    ffn_tok = dot((at == row).astype(jnp.bfloat16), home[...])
    expert_out[...] = (as_column(gate[...]) * ffn_tok).astype(jnp.bfloat16)
    gate_grad[...] = as_row(jnp.sum(out_grad[...].astype(jnp.float32) * ffn_tok, axis=1, keepdims=True))
    token_grad[...] = dot((at == row + CAP).astype(jnp.bfloat16), home[...]).astype(jnp.bfloat16)


def row_order(wide, kind_first, transposed):
    part_rows = wide // TILE * CAP
    shape = (wide, wide)
    index = lax.broadcasted_iota(jnp.int32, shape, 1 if transposed else 0)
    at = lax.broadcasted_iota(jnp.int32, shape, 0 if transposed else 1)
    part = sum((index >= part_rows * k).astype(jnp.int32) for k in range(1, EGRP * KINDS))
    within = index - part * part_rows
    if kind_first:
        part = (part & 1) * KINDS + (part >> 1)
    return (at == (within >> 1) * TILE + part * CAP + (within & 1)).astype(jnp.bfloat16)


def encode(value):
    size = jnp.abs(value)
    code = jnp.round((jnp.log2(jnp.maximum(size, SMALLEST)) + OCTAVES) * STEPS)
    code = jnp.where(size < SMALLEST, 0.0, code)
    return jnp.where(value < 0.0, -code, code).astype(jnp.int32).astype(jnp.int16)


def decode(code):
    wide = code.astype(jnp.int32).astype(jnp.float32)
    value = jnp.exp2(jnp.abs(wide) * (1.0 / STEPS) - OCTAVES)
    return jnp.where(wide < 0.0, -value, value).astype(jnp.bfloat16)


def order_kernel(rows, codes_x, rows_g):
    moved = dot(row_order(rows.shape[0], True, False), rows[...])
    half = rows.shape[0] // KINDS
    codes_x[...] = encode(moved[:half])
    rows_g[...] = moved[half:].astype(jnp.bfloat16)


def restore_kernel(rows, restored):
    restored[...] = dot(row_order(rows.shape[0], False, True), rows[...]).astype(jnp.bfloat16)


def flat(rows):
    sources, count, width = rows.shape
    return rows.reshape(sources * count, width)


def forward_rows(codes_x, rows_g, weight_in, weight_out):
    rows_x = flat(decode(codes_x[...]))
    rows_g = flat(rows_g[...])
    pre_act = dot(rows_x, weight_in[...])
    hidden_grad = dot(rows_g, weight_out[...], ((1,), (1,)))
    value, slope = gelu_and_slope(pre_act)
    return rows_x, rows_g, value.astype(jnp.bfloat16), (hidden_grad * slope).astype(jnp.bfloat16)


def expert_kernel(group_ref, codes_x, rows_g, weight_in, weight_out, send):
    sources, part, width = codes_x.shape
    _, _, hidden, pre_grad = forward_rows(codes_x, rows_g, weight_in, weight_out)
    part_out = dot(hidden, weight_out[...]).astype(jnp.bfloat16)
    part_in = dot(pre_grad, weight_in[...], ((1,), (1,))).astype(jnp.bfloat16)
    narrow = KINDS * part
    own = pl.multiple_of(group_ref[0] * narrow, narrow)
    other = pl.multiple_of((EGRP - 1 - group_ref[0]) * narrow, narrow)
    send[:, pl.ds(other, narrow), :] = jnp.zeros((sources, narrow, width), jnp.bfloat16)
    send[:, pl.ds(own, part), :] = part_out.reshape(sources, part, width)
    send[:, pl.ds(own + part, part), :] = part_in.reshape(sources, part, width)


def weights_kernel(group_ref, codes_x, rows_g, weight_in, weight_out, grad_in, grad_out, sum_in, sum_out):
    rows_x, rows_g, hidden, pre_grad = forward_rows(codes_x, rows_g, weight_in, weight_out)

    @pl.when(pl.program_id(0) == 0)
    def _():
        sum_in[...] = jnp.zeros_like(sum_in)
        sum_out[...] = jnp.zeros_like(sum_out)

    sum_in[...] += dot(rows_x, pre_grad, ((0,), (0,)))
    sum_out[...] += dot(hidden, rows_g, ((0,), (0,)))

    @pl.when(pl.program_id(0) == pl.num_programs(0) - 1)
    def _():
        grad_in[...] = sum_in[...].astype(grad_in.dtype)
        grad_out[...] = sum_out[...].astype(grad_out.dtype)


def on_device(tokens, expert_ids, slot_ids, keep_mask, gate_prob, out_grad, in_weight, out_weight):
    tok_rows, width = tokens.shape
    intra_size = lax.axis_size("intra")
    inter_size = lax.axis_size("inter")
    blocks_ff = inter_size // EGRP
    group = (lax.axis_index("inter") // blocks_ff).astype(jnp.int32).reshape(1)
    weight_in = in_weight[0, 0]
    weight_out = out_weight[0, 0]
    hidden_units = weight_in.shape[1]
    wide = intra_size * TILE
    params = pltpu.CompilerParams(vmem_limit_bytes=VMEM_BYTES)
    small = pltpu.CompilerParams(vmem_limit_bytes=VMEM_SMALL)
    routing = (expert_ids[None], slot_ids[None], keep_mask[None], gate_prob[None])

    placed = pl.pallas_call(
        functools.partial(place_kernel, intra_size),
        out_shape=jax.ShapeDtypeStruct((wide, width), jnp.bfloat16),
        compiler_params=params,
        name="place",
    )(tokens, *routing, out_grad)
    moved = lax.all_to_all(placed.reshape(intra_size, TILE, width), "intra", 0, 0, tiled=True)
    part = wide // (EGRP * KINDS)
    ordered_x, ordered_g = pl.pallas_call(
        order_kernel,
        out_shape=[
            jax.ShapeDtypeStruct((EGRP * part, width), jnp.int16),
            jax.ShapeDtypeStruct((EGRP * part, width), jnp.bfloat16),
        ],
        compiler_params=small,
        name="order",
    )(moved.reshape(wide, width))
    spread_g = lax.all_gather(ordered_g[None], "inter", axis=0, tiled=True)
    spread_x = lax.all_gather(ordered_x[None], "inter", axis=0, tiled=True)

    step = 4
    whole = lambda i, group_ref: (0, 0)
    by_plane = pl.BlockSpec((step, wide, width), lambda i, group_ref: (i, 0, 0))
    own_rows = pl.BlockSpec((step, part, width), lambda i, group_ref: (i, group_ref[0], 0))
    in_block = pl.BlockSpec((width, hidden_units), whole)
    out_block = pl.BlockSpec((hidden_units, width), whole)

    def over_planes(kernel, name, out_specs, out_shape, scratch):
        return pl.pallas_call(
            kernel,
            grid_spec=pltpu.PrefetchScalarGridSpec(
                num_scalar_prefetch=1,
                grid=(inter_size // step,),
                in_specs=[own_rows, own_rows, in_block, out_block],
                out_specs=out_specs,
                scratch_shapes=scratch,
            ),
            out_shape=out_shape,
            compiler_params=params,
            name=name,
        )(group, spread_x, spread_g, weight_in, weight_out)

    send = over_planes(
        expert_kernel, "expert", by_plane, jax.ShapeDtypeStruct((inter_size, wide, width), jnp.bfloat16), []
    )
    summed = lax.psum_scatter(send, "inter", scatter_dimension=0, tiled=True)
    in_weight_grad, out_weight_grad = over_planes(
        weights_kernel,
        "weight_grads",
        [in_block, out_block],
        [jax.ShapeDtypeStruct(w.shape, jnp.bfloat16) for w in (weight_in, weight_out)],
        [pltpu.VMEM(w.shape, jnp.float32) for w in (weight_in, weight_out)],
    )
    summed, out_weight_grad, in_weight_grad = lax.optimization_barrier((summed, out_weight_grad, in_weight_grad))

    back = pl.pallas_call(
        restore_kernel,
        out_shape=jax.ShapeDtypeStruct((wide, width), jnp.bfloat16),
        compiler_params=small,
        name="restore",
    )(summed.reshape(wide, width))
    home = lax.all_to_all(back.reshape(intra_size, TILE, width), "intra", 0, 0, tiled=True)
    expert_out, gate_grad, token_grad = pl.pallas_call(
        functools.partial(pick_kernel, intra_size),
        out_shape=[
            jax.ShapeDtypeStruct((tok_rows, width), jnp.bfloat16),
            jax.ShapeDtypeStruct((1, tok_rows), jnp.float32),
            jax.ShapeDtypeStruct((tok_rows, width), jnp.bfloat16),
        ],
        compiler_params=small,
        name="pick",
    )(home.reshape(wide, width), *routing, out_grad)
    return (
        expert_out,
        gate_grad.reshape(tok_rows),
        token_grad,
        in_weight_grad[None, None],
        out_weight_grad[None, None],
    )


def solution(mesh):
    tok = P(("inter", "intra"), None)
    per = P(("inter", "intra"))
    wgt = P("inter", "intra", None, None)
    return jax.shard_map(
        on_device,
        mesh=mesh,
        in_specs=(tok, per, per, per, per, tok, wgt, wgt),
        out_specs=(tok, per, tok, wgt, wgt),
        check_vma=False,
    )
```

```python
import functools
import math

import jax
import jax.numpy as jnp
from jax import lax
from jax.experimental import pallas as pl
from jax.experimental.pallas import tpu as pltpu
from jax.sharding import PartitionSpec as P

EGRP = 2
CAP = 2
KINDS = 2
TILE = EGRP * KINDS * CAP
VMEM_BYTES = 60 * 1024 * 1024
VMEM_SMALL = 8 * 1024 * 1024
TAIL = 128
STEPS = 229.0
OCTAVES = 140.0
SMALLEST = 2.0**-126

gelu_root = math.sqrt(2.0 / math.pi)
gelu_cubic = 0.044715


def gelu_and_slope(pre_value):
    square = pre_value * pre_value
    argument = gelu_root * (pre_value + gelu_cubic * square * pre_value)
    slope_tanh = jnp.tanh(argument)
    half_up = 0.5 * (1.0 + slope_tanh)
    value = pre_value * half_up
    slope = half_up + 0.5 * pre_value * (1.0 - slope_tanh * slope_tanh) * gelu_root * (
        1.0 + 3.0 * gelu_cubic * square
    )
    return value, slope


def dot(left, right, dims=((1,), (0,))):
    return lax.dot_general(left, right, (dims, ((), ())), preferred_element_type=jnp.float32)


def slot_row(experts, slots, keep, intra_size):
    group = (experts >= intra_size).astype(jnp.int32)
    row = (experts - group * intra_size) * TILE + group * (KINDS * CAP) + slots
    return jnp.where(keep == 1, row, -TILE)


def as_column(row):
    count = row.shape[1]
    shape = (count, count)
    diagonal = lax.broadcasted_iota(jnp.int32, shape, 0) == lax.broadcasted_iota(jnp.int32, shape, 1)
    return jnp.sum(jnp.where(diagonal, row, 0.0), axis=1, keepdims=True)


def as_row(column):
    count = column.shape[0]
    shape = (count, count)
    diagonal = lax.broadcasted_iota(jnp.int32, shape, 0) == lax.broadcasted_iota(jnp.int32, shape, 1)
    return jnp.sum(jnp.where(diagonal, column, 0.0), axis=0, keepdims=True)


def place_kernel(intra_size, tokens, experts, slots, keep, gate, out_grad, send):
    count = tokens.shape[0]
    row = slot_row(experts[...], slots[...], keep[...], intra_size)
    scaled = (as_column(gate[...]) * out_grad[...].astype(jnp.float32)).astype(jnp.bfloat16)
    at = lax.broadcasted_iota(jnp.int32, (send.shape[0], count), 0)
    hot_x = (at == row).astype(jnp.bfloat16)
    hot_g = (at == row + CAP).astype(jnp.bfloat16)
    send[...] = (dot(hot_x, tokens[...]) + dot(hot_g, scaled)).astype(jnp.bfloat16)


def pick_kernel(intra_size, home, experts, slots, keep, gate, out_grad, expert_out, gate_grad, token_grad):
    count = out_grad.shape[0]
    row = slot_row(experts[...], slots[...], keep[...], intra_size)
    row = as_column(row.astype(jnp.float32)).astype(jnp.int32)
    at = lax.broadcasted_iota(jnp.int32, (count, home.shape[0]), 1)
    ffn_tok = dot((at == row).astype(jnp.bfloat16), home[...])
    expert_out[...] = (as_column(gate[...]) * ffn_tok).astype(jnp.bfloat16)
    gate_grad[...] = as_row(jnp.sum(out_grad[...].astype(jnp.float32) * ffn_tok, axis=1, keepdims=True))
    token_grad[...] = dot((at == row + CAP).astype(jnp.bfloat16), home[...]).astype(jnp.bfloat16)


def row_order(wide, kind_first, transposed):
    part_rows = wide // TILE * CAP
    shape = (wide, wide)
    index = lax.broadcasted_iota(jnp.int32, shape, 1 if transposed else 0)
    at = lax.broadcasted_iota(jnp.int32, shape, 0 if transposed else 1)
    part = sum((index >= part_rows * k).astype(jnp.int32) for k in range(1, EGRP * KINDS))
    within = index - part * part_rows
    if kind_first:
        part = (part & 1) * KINDS + (part >> 1)
    return (at == (within >> 1) * TILE + part * CAP + (within & 1)).astype(jnp.bfloat16)


def encode(value):
    size = jnp.abs(value)
    code = jnp.round((jnp.log2(jnp.maximum(size, SMALLEST)) + OCTAVES) * STEPS)
    code = jnp.where(size < SMALLEST, 0.0, code)
    return jnp.where(value < 0.0, -code, code).astype(jnp.int32).astype(jnp.int16)


def decode(code):
    wide = code.astype(jnp.int32).astype(jnp.float32)
    value = jnp.exp2(jnp.abs(wide) * (1.0 / STEPS) - OCTAVES)
    return jnp.where(wide < 0.0, -value, value).astype(jnp.bfloat16)


def order_gradients_kernel(rows, rows_g):
    order = row_order(rows.shape[0], True, False)[rows.shape[0] // KINDS :]
    rows_g[...] = dot(order, rows[:, : rows_g.shape[1]]).astype(jnp.bfloat16)


def order_codes_kernel(rows, codes):
    count, width = rows.shape
    moved = dot(row_order(count, True, False), rows[...])
    codes[:, :width] = encode(moved[: count // KINDS])
    codes[:, width:] = encode(moved[count // KINDS :, width - TAIL :])


def restore_kernel(rows, restored):
    restored[...] = dot(row_order(rows.shape[0], False, True), rows[...]).astype(jnp.bfloat16)


def flat(rows):
    sources, count, width = rows.shape
    return rows.reshape(sources * count, width)


def forward_rows(codes, rows_g, weight_in, weight_out):
    width = weight_in.shape[0]
    decoded = decode(flat(codes[...]))
    rows_x = decoded[:, :width]
    rows_g = jnp.concatenate([flat(rows_g[...]), decoded[:, width:]], axis=1)
    pre_act = dot(rows_x, weight_in[...])
    hidden_grad = dot(rows_g, weight_out[...], ((1,), (1,)))
    value, slope = gelu_and_slope(pre_act)
    return rows_x, rows_g, value.astype(jnp.bfloat16), (hidden_grad * slope).astype(jnp.bfloat16)


def expert_kernel(group_ref, codes, rows_g, weight_in, weight_out, send):
    sources, part, _ = codes.shape
    width = send.shape[2]
    _, _, hidden, pre_grad = forward_rows(codes, rows_g, weight_in, weight_out)
    part_out = dot(hidden, weight_out[...]).astype(jnp.bfloat16)
    part_in = dot(pre_grad, weight_in[...], ((1,), (1,))).astype(jnp.bfloat16)
    narrow = KINDS * part
    own = pl.multiple_of(group_ref[0] * narrow, narrow)
    other = pl.multiple_of((EGRP - 1 - group_ref[0]) * narrow, narrow)
    send[:, pl.ds(other, narrow), :] = jnp.zeros((sources, narrow, width), jnp.bfloat16)
    send[:, pl.ds(own, part), :] = part_out.reshape(sources, part, width)
    send[:, pl.ds(own + part, part), :] = part_in.reshape(sources, part, width)


def weights_kernel(group_ref, codes, rows_g, weight_in, weight_out, grad_in, grad_out, sum_in, sum_out):
    rows_x, rows_g, hidden, pre_grad = forward_rows(codes, rows_g, weight_in, weight_out)

    @pl.when(pl.program_id(0) == 0)
    def _():
        sum_in[...] = jnp.zeros_like(sum_in)
        sum_out[...] = jnp.zeros_like(sum_out)

    sum_in[...] += dot(rows_x, pre_grad, ((0,), (0,)))
    sum_out[...] += dot(hidden, rows_g, ((0,), (0,)))

    @pl.when(pl.program_id(0) == pl.num_programs(0) - 1)
    def _():
        grad_in[...] = sum_in[...].astype(grad_in.dtype)
        grad_out[...] = sum_out[...].astype(grad_out.dtype)


def on_device(tokens, expert_ids, slot_ids, keep_mask, gate_prob, out_grad, in_weight, out_weight):
    tok_rows, width = tokens.shape
    intra_size = lax.axis_size("intra")
    inter_size = lax.axis_size("inter")
    blocks_ff = inter_size // EGRP
    group = (lax.axis_index("inter") // blocks_ff).astype(jnp.int32).reshape(1)
    weight_in = in_weight[0, 0]
    weight_out = out_weight[0, 0]
    hidden_units = weight_in.shape[1]
    wide = intra_size * TILE
    params = pltpu.CompilerParams(vmem_limit_bytes=VMEM_BYTES)
    small = pltpu.CompilerParams(vmem_limit_bytes=VMEM_SMALL)
    routing = (expert_ids[None], slot_ids[None], keep_mask[None], gate_prob[None])

    placed = pl.pallas_call(
        functools.partial(place_kernel, intra_size),
        out_shape=jax.ShapeDtypeStruct((wide, width), jnp.bfloat16),
        compiler_params=params,
        name="place",
    )(tokens, *routing, out_grad)
    moved = lax.all_to_all(placed.reshape(intra_size, TILE, width), "intra", 0, 0, tiled=True)
    part = wide // (EGRP * KINDS)
    half = EGRP * part

    def order(kernel, name, columns, dtype):
        return pl.pallas_call(
            kernel,
            out_shape=jax.ShapeDtypeStruct((half, columns), dtype),
            compiler_params=small,
            name=name,
        )(moved.reshape(wide, width))

    ordered_g = order(order_gradients_kernel, "order_gradients", width - TAIL, jnp.bfloat16)
    ordered_x = order(order_codes_kernel, "order_codes", width + TAIL, jnp.int16)
    spread_g = lax.all_gather(ordered_g[None], "inter", axis=0, tiled=True)
    spread_x = lax.all_gather(ordered_x[None], "inter", axis=0, tiled=True)

    step = 4
    whole = lambda i, group_ref: (0, 0)
    by_plane = pl.BlockSpec((step, wide, width), lambda i, group_ref: (i, 0, 0))
    own = lambda columns: pl.BlockSpec((step, part, columns), lambda i, group_ref: (i, group_ref[0], 0))
    in_block = pl.BlockSpec((width, hidden_units), whole)
    out_block = pl.BlockSpec((hidden_units, width), whole)

    def over_planes(kernel, name, out_specs, out_shape, scratch):
        return pl.pallas_call(
            kernel,
            grid_spec=pltpu.PrefetchScalarGridSpec(
                num_scalar_prefetch=1,
                grid=(inter_size // step,),
                in_specs=[own(width + TAIL), own(width - TAIL), in_block, out_block],
                out_specs=out_specs,
                scratch_shapes=scratch,
            ),
            out_shape=out_shape,
            compiler_params=params,
            name=name,
        )(group, spread_x, spread_g, weight_in, weight_out)

    send = over_planes(
        expert_kernel, "expert", by_plane, jax.ShapeDtypeStruct((inter_size, wide, width), jnp.bfloat16), []
    )
    summed = lax.psum_scatter(send, "inter", scatter_dimension=0, tiled=True)
    in_weight_grad, out_weight_grad = over_planes(
        weights_kernel,
        "weight_grads",
        [in_block, out_block],
        [jax.ShapeDtypeStruct(w.shape, jnp.bfloat16) for w in (weight_in, weight_out)],
        [pltpu.VMEM(w.shape, jnp.float32) for w in (weight_in, weight_out)],
    )
    summed, out_weight_grad, in_weight_grad = lax.optimization_barrier((summed, out_weight_grad, in_weight_grad))

    back = pl.pallas_call(
        restore_kernel,
        out_shape=jax.ShapeDtypeStruct((wide, width), jnp.bfloat16),
        compiler_params=small,
        name="restore",
    )(summed.reshape(wide, width))
    home = lax.all_to_all(back.reshape(intra_size, TILE, width), "intra", 0, 0, tiled=True)
    expert_out, gate_grad, token_grad = pl.pallas_call(
        functools.partial(pick_kernel, intra_size),
        out_shape=[
            jax.ShapeDtypeStruct((tok_rows, width), jnp.bfloat16),
            jax.ShapeDtypeStruct((1, tok_rows), jnp.float32),
            jax.ShapeDtypeStruct((tok_rows, width), jnp.bfloat16),
        ],
        compiler_params=small,
        name="pick",
    )(home.reshape(wide, width), *routing, out_grad)
    return (
        expert_out,
        gate_grad.reshape(tok_rows),
        token_grad,
        in_weight_grad[None, None],
        out_weight_grad[None, None],
    )


def solution(mesh):
    tok = P(("inter", "intra"), None)
    per = P(("inter", "intra"))
    wgt = P("inter", "intra", None, None)
    return jax.shard_map(
        on_device,
        mesh=mesh,
        in_specs=(tok, per, per, per, per, tok, wgt, wgt),
        out_specs=(tok, per, tok, wgt, wgt),
        check_vma=False,
    )
```

```python
import functools
import math

import jax
import jax.numpy as jnp
from jax import lax
from jax.experimental import pallas as pl
from jax.experimental.pallas import tpu as pltpu
from jax.sharding import PartitionSpec as P

EGRP = 2
CAP = 2
KINDS = 2
TILE = EGRP * KINDS * CAP
VMEM_BYTES = 60 * 1024 * 1024
VMEM_SMALL = 8 * 1024 * 1024
VMEM_MOST = 52 * 1024 * 1024
TAIL = 128
STEPS = 229.0
OCTAVES = 140.0
SMALLEST = 2.0**-126

gelu_root = math.sqrt(2.0 / math.pi)
gelu_cubic = 0.044715


def gelu_and_slope(pre_value):
    square = pre_value * pre_value
    argument = gelu_root * (pre_value + gelu_cubic * square * pre_value)
    slope_tanh = jnp.tanh(argument)
    half_up = 0.5 * (1.0 + slope_tanh)
    value = pre_value * half_up
    slope = half_up + 0.5 * pre_value * (1.0 - slope_tanh * slope_tanh) * gelu_root * (
        1.0 + 3.0 * gelu_cubic * square
    )
    return value, slope


def dot(left, right, dims=((1,), (0,))):
    return lax.dot_general(left, right, (dims, ((), ())), preferred_element_type=jnp.float32)


def slot_row(experts, slots, keep, intra_size):
    group = (experts >= intra_size).astype(jnp.int32)
    row = (experts - group * intra_size) * TILE + group * (KINDS * CAP) + slots
    return jnp.where(keep == 1, row, -TILE)


def as_column(row):
    count = row.shape[1]
    shape = (count, count)
    diagonal = lax.broadcasted_iota(jnp.int32, shape, 0) == lax.broadcasted_iota(jnp.int32, shape, 1)
    return jnp.sum(jnp.where(diagonal, row, 0.0), axis=1, keepdims=True)


def as_row(column):
    count = column.shape[0]
    shape = (count, count)
    diagonal = lax.broadcasted_iota(jnp.int32, shape, 0) == lax.broadcasted_iota(jnp.int32, shape, 1)
    return jnp.sum(jnp.where(diagonal, column, 0.0), axis=0, keepdims=True)


def place_kernel(intra_size, tokens, experts, slots, keep, gate, out_grad, send):
    count = tokens.shape[0]
    row = slot_row(experts[...], slots[...], keep[...], intra_size)
    scaled = (as_column(gate[...]) * out_grad[...].astype(jnp.float32)).astype(jnp.bfloat16)
    at = lax.broadcasted_iota(jnp.int32, (send.shape[0], count), 0)
    hot_x = (at == row).astype(jnp.bfloat16)
    hot_g = (at == row + CAP).astype(jnp.bfloat16)
    send[...] = (dot(hot_x, tokens[...]) + dot(hot_g, scaled)).astype(jnp.bfloat16)


def pick_kernel(intra_size, home, experts, slots, keep, gate, out_grad, expert_out, gate_grad, token_grad):
    count = out_grad.shape[0]
    row = slot_row(experts[...], slots[...], keep[...], intra_size)
    row = as_column(row.astype(jnp.float32)).astype(jnp.int32)
    at = lax.broadcasted_iota(jnp.int32, (count, home.shape[0]), 1)
    ffn_tok = dot((at == row).astype(jnp.bfloat16), home[...])
    expert_out[...] = (as_column(gate[...]) * ffn_tok).astype(jnp.bfloat16)
    gate_grad[...] = as_row(jnp.sum(out_grad[...].astype(jnp.float32) * ffn_tok, axis=1, keepdims=True))
    token_grad[...] = dot((at == row + CAP).astype(jnp.bfloat16), home[...]).astype(jnp.bfloat16)


def row_order(wide, kind_first, transposed):
    part_rows = wide // TILE * CAP
    shape = (wide, wide)
    index = lax.broadcasted_iota(jnp.int32, shape, 1 if transposed else 0)
    at = lax.broadcasted_iota(jnp.int32, shape, 0 if transposed else 1)
    part = sum((index >= part_rows * k).astype(jnp.int32) for k in range(1, EGRP * KINDS))
    within = index - part * part_rows
    if kind_first:
        part = (part & 1) * KINDS + (part >> 1)
    return (at == (within >> 1) * TILE + part * CAP + (within & 1)).astype(jnp.bfloat16)


def encode(value):
    size = jnp.abs(value)
    code = jnp.round((jnp.log2(jnp.maximum(size, SMALLEST)) + OCTAVES) * STEPS)
    code = jnp.where(size < SMALLEST, 0.0, code)
    return jnp.where(value < 0.0, -code, code).astype(jnp.int32).astype(jnp.int16)


def decode(code):
    wide = code.astype(jnp.int32).astype(jnp.float32)
    value = jnp.exp2(jnp.abs(wide) * (1.0 / STEPS) - OCTAVES)
    return jnp.where(wide < 0.0, -value, value).astype(jnp.bfloat16)


def order_gradients_kernel(rows, rows_g):
    order = row_order(rows.shape[0], True, False)[rows.shape[0] // KINDS :]
    rows_g[...] = dot(order, rows[:, : rows_g.shape[1]]).astype(jnp.bfloat16)


def order_codes_kernel(rows, codes):
    count, width = rows.shape
    moved = dot(row_order(count, True, False), rows[...])
    codes[:, :width] = encode(moved[: count // KINDS])
    codes[:, width:] = encode(moved[count // KINDS :, width - TAIL :])


def restore_kernel(rows, restored):
    restored[...] = dot(row_order(rows.shape[0], False, True), rows[...]).astype(jnp.bfloat16)


def flat(rows):
    sources, count, width = rows.shape
    return rows.reshape(sources * count, width)


def forward_rows(codes, rows_g, weight_in, weight_out):
    width = weight_in.shape[0]
    decoded = decode(flat(codes[...]))
    rows_x = decoded[:, :width]
    rows_g = jnp.concatenate([flat(rows_g[...]), decoded[:, width:]], axis=1)
    pre_act = dot(rows_x, weight_in[...])
    hidden_grad = dot(rows_g, weight_out[...], ((1,), (1,)))
    value, slope = gelu_and_slope(pre_act)
    return rows_x, rows_g, value.astype(jnp.bfloat16), (hidden_grad * slope).astype(jnp.bfloat16)


def expert_kernel(group_ref, codes, rows_g, weight_in, weight_out, send):
    sources, part, _ = codes.shape
    width = send.shape[2]
    _, _, hidden, pre_grad = forward_rows(codes, rows_g, weight_in, weight_out)
    part_out = dot(hidden, weight_out[...]).astype(jnp.bfloat16)
    part_in = dot(pre_grad, weight_in[...], ((1,), (1,))).astype(jnp.bfloat16)
    narrow = KINDS * part
    own = pl.multiple_of(group_ref[0] * narrow, narrow)
    other = pl.multiple_of((EGRP - 1 - group_ref[0]) * narrow, narrow)
    send[:, pl.ds(other, narrow), :] = jnp.zeros((sources, narrow, width), jnp.bfloat16)
    send[:, pl.ds(own, part), :] = part_out.reshape(sources, part, width)
    send[:, pl.ds(own + part, part), :] = part_in.reshape(sources, part, width)


def weights_kernel(group_ref, codes, rows_g, weight_in, weight_out, grad_in, grad_out, sum_in, sum_out):
    rows_x, rows_g, hidden, pre_grad = forward_rows(codes, rows_g, weight_in, weight_out)

    @pl.when(pl.program_id(0) == 0)
    def _():
        sum_in[...] = jnp.zeros_like(sum_in)
        sum_out[...] = jnp.zeros_like(sum_out)

    sum_in[...] += dot(rows_x, pre_grad, ((0,), (0,)))
    sum_out[...] += dot(hidden, rows_g, ((0,), (0,)))

    @pl.when(pl.program_id(0) == pl.num_programs(0) - 1)
    def _():
        grad_in[...] = sum_in[...].astype(grad_in.dtype)
        grad_out[...] = sum_out[...].astype(grad_out.dtype)


def on_device(tokens, expert_ids, slot_ids, keep_mask, gate_prob, out_grad, in_weight, out_weight):
    tok_rows, width = tokens.shape
    intra_size = lax.axis_size("intra")
    inter_size = lax.axis_size("inter")
    blocks_ff = inter_size // EGRP
    group = (lax.axis_index("inter") // blocks_ff).astype(jnp.int32).reshape(1)
    weight_in = in_weight[0, 0]
    weight_out = out_weight[0, 0]
    hidden_units = weight_in.shape[1]
    wide = intra_size * TILE
    params = pltpu.CompilerParams(vmem_limit_bytes=VMEM_BYTES)
    small = pltpu.CompilerParams(vmem_limit_bytes=VMEM_SMALL)
    routing = (expert_ids[None], slot_ids[None], keep_mask[None], gate_prob[None])

    placed = pl.pallas_call(
        functools.partial(place_kernel, intra_size),
        out_shape=jax.ShapeDtypeStruct((wide, width), jnp.bfloat16),
        compiler_params=params,
        name="place",
    )(tokens, *routing, out_grad)
    moved = lax.all_to_all(placed.reshape(intra_size, TILE, width), "intra", 0, 0, tiled=True)
    part = wide // (EGRP * KINDS)
    half = EGRP * part

    def order(kernel, name, columns, dtype):
        return pl.pallas_call(
            kernel,
            out_shape=jax.ShapeDtypeStruct((half, columns), dtype),
            compiler_params=small,
            name=name,
        )(moved.reshape(wide, width))

    ordered_g = order(order_gradients_kernel, "order_gradients", width - TAIL, jnp.bfloat16)
    ordered_x = order(order_codes_kernel, "order_codes", width + TAIL, jnp.int16)
    spread_g = lax.all_gather(ordered_g[None], "inter", axis=0, tiled=True)
    spread_x = lax.all_gather(ordered_x[None], "inter", axis=0, tiled=True)

    step = 4
    whole = lambda i, group_ref: (0, 0)
    by_plane = pl.BlockSpec((step, wide, width), lambda i, group_ref: (i, 0, 0))
    own = lambda columns: pl.BlockSpec((step, part, columns), lambda i, group_ref: (i, group_ref[0], 0))
    in_block = pl.BlockSpec((width, hidden_units), whole)
    out_block = pl.BlockSpec((hidden_units, width), whole)

    def over_planes(kernel, name, out_specs, out_shape, scratch, grant=VMEM_BYTES):
        return pl.pallas_call(
            kernel,
            grid_spec=pltpu.PrefetchScalarGridSpec(
                num_scalar_prefetch=1,
                grid=(inter_size // step,),
                in_specs=[own(width + TAIL), own(width - TAIL), in_block, out_block],
                out_specs=out_specs,
                scratch_shapes=scratch,
            ),
            out_shape=out_shape,
            compiler_params=pltpu.CompilerParams(vmem_limit_bytes=grant),
            name=name,
        )(group, spread_x, spread_g, weight_in, weight_out)

    send = over_planes(
        expert_kernel, "expert", by_plane, jax.ShapeDtypeStruct((inter_size, wide, width), jnp.bfloat16), [], VMEM_MOST
    )
    summed = lax.psum_scatter(send, "inter", scatter_dimension=0, tiled=True)
    in_weight_grad, out_weight_grad = over_planes(
        weights_kernel,
        "weight_grads",
        [in_block, out_block],
        [jax.ShapeDtypeStruct(w.shape, jnp.bfloat16) for w in (weight_in, weight_out)],
        [pltpu.VMEM(w.shape, jnp.float32) for w in (weight_in, weight_out)],
    )
    summed, out_weight_grad, in_weight_grad = lax.optimization_barrier((summed, out_weight_grad, in_weight_grad))

    back = pl.pallas_call(
        restore_kernel,
        out_shape=jax.ShapeDtypeStruct((wide, width), jnp.bfloat16),
        compiler_params=small,
        name="restore",
    )(summed.reshape(wide, width))
    home = lax.all_to_all(back.reshape(intra_size, TILE, width), "intra", 0, 0, tiled=True)
    expert_out, gate_grad, token_grad = pl.pallas_call(
        functools.partial(pick_kernel, intra_size),
        out_shape=[
            jax.ShapeDtypeStruct((tok_rows, width), jnp.bfloat16),
            jax.ShapeDtypeStruct((1, tok_rows), jnp.float32),
            jax.ShapeDtypeStruct((tok_rows, width), jnp.bfloat16),
        ],
        compiler_params=small,
        name="pick",
    )(home.reshape(wide, width), *routing, out_grad)
    return (
        expert_out,
        gate_grad.reshape(tok_rows),
        token_grad,
        in_weight_grad[None, None],
        out_weight_grad[None, None],
    )


def solution(mesh):
    tok = P(("inter", "intra"), None)
    per = P(("inter", "intra"))
    wgt = P("inter", "intra", None, None)
    return jax.shard_map(
        on_device,
        mesh=mesh,
        in_specs=(tok, per, per, per, per, tok, wgt, wgt),
        out_specs=(tok, per, tok, wgt, wgt),
        check_vma=False,
    )
```

```python
import functools
import math

import jax
import jax.numpy as jnp
from jax import lax
from jax.experimental import pallas as pl
from jax.experimental.pallas import tpu as pltpu
from jax.sharding import PartitionSpec as P

EGRP = 2
CAP = 2
KINDS = 2
TILE = EGRP * KINDS * CAP
VMEM_BYTES = 60 * 1024 * 1024
VMEM_SMALL = 8 * 1024 * 1024
VMEM_MOST = 52 * 1024 * 1024
TAIL = 128
STEPS = 229.0
OCTAVES = 140.0
SMALLEST = 2.0**-126

gelu_root = math.sqrt(2.0 / math.pi)
gelu_cubic = 0.044715


def gelu_and_slope(pre_value):
    square = pre_value * pre_value
    argument = gelu_root * (pre_value + gelu_cubic * square * pre_value)
    slope_tanh = jnp.tanh(argument)
    half_up = 0.5 * (1.0 + slope_tanh)
    value = pre_value * half_up
    slope = half_up + 0.5 * pre_value * (1.0 - slope_tanh * slope_tanh) * gelu_root * (
        1.0 + 3.0 * gelu_cubic * square
    )
    return value, slope


def dot(left, right, dims=((1,), (0,))):
    return lax.dot_general(left, right, (dims, ((), ())), preferred_element_type=jnp.float32)


def slot_row(experts, slots, keep, intra_size):
    group = (experts >= intra_size).astype(jnp.int32)
    row = (experts - group * intra_size) * TILE + group * (KINDS * CAP) + slots
    return jnp.where(keep == 1, row, -TILE)


def as_column(row):
    count = row.shape[1]
    shape = (count, count)
    diagonal = lax.broadcasted_iota(jnp.int32, shape, 0) == lax.broadcasted_iota(jnp.int32, shape, 1)
    return jnp.sum(jnp.where(diagonal, row, 0.0), axis=1, keepdims=True)


def as_row(column):
    count = column.shape[0]
    shape = (count, count)
    diagonal = lax.broadcasted_iota(jnp.int32, shape, 0) == lax.broadcasted_iota(jnp.int32, shape, 1)
    return jnp.sum(jnp.where(diagonal, column, 0.0), axis=0, keepdims=True)


def place_kernel(intra_size, tokens, experts, slots, keep, gate, out_grad, send):
    count = tokens.shape[0]
    row = slot_row(experts[...], slots[...], keep[...], intra_size)
    scaled = (as_column(gate[...]) * out_grad[...].astype(jnp.float32)).astype(jnp.bfloat16)
    at = lax.broadcasted_iota(jnp.int32, (send.shape[0], count), 0)
    hot_x = (at == row).astype(jnp.bfloat16)
    hot_g = (at == row + CAP).astype(jnp.bfloat16)
    send[...] = (dot(hot_x, tokens[...]) + dot(hot_g, scaled)).astype(jnp.bfloat16)


def pick_kernel(intra_size, home, experts, slots, keep, gate, out_grad, expert_out, gate_grad, token_grad):
    count = out_grad.shape[0]
    row = slot_row(experts[...], slots[...], keep[...], intra_size)
    row = as_column(row.astype(jnp.float32)).astype(jnp.int32)
    at = lax.broadcasted_iota(jnp.int32, (count, home.shape[0]), 1)
    ffn_tok = dot((at == row).astype(jnp.bfloat16), home[...])
    expert_out[...] = (as_column(gate[...]) * ffn_tok).astype(jnp.bfloat16)
    gate_grad[...] = as_row(jnp.sum(out_grad[...].astype(jnp.float32) * ffn_tok, axis=1, keepdims=True))
    token_grad[...] = dot((at == row + CAP).astype(jnp.bfloat16), home[...]).astype(jnp.bfloat16)


def row_order(wide, kind_first, transposed):
    part_rows = wide // TILE * CAP
    shape = (wide, wide)
    index = lax.broadcasted_iota(jnp.int32, shape, 1 if transposed else 0)
    at = lax.broadcasted_iota(jnp.int32, shape, 0 if transposed else 1)
    part = sum((index >= part_rows * k).astype(jnp.int32) for k in range(1, EGRP * KINDS))
    within = index - part * part_rows
    if kind_first:
        part = (part & 1) * KINDS + (part >> 1)
    return (at == (within >> 1) * TILE + part * CAP + (within & 1)).astype(jnp.bfloat16)


def encode(value):
    size = jnp.abs(value)
    code = jnp.round((jnp.log2(jnp.maximum(size, SMALLEST)) + OCTAVES) * STEPS)
    code = jnp.where(size < SMALLEST, 0.0, code)
    return jnp.where(value < 0.0, -code, code).astype(jnp.int32).astype(jnp.int16)


def decode(code):
    wide = code.astype(jnp.int32).astype(jnp.float32)
    value = jnp.exp2(jnp.abs(wide) * (1.0 / STEPS) - OCTAVES)
    return jnp.where(wide < 0.0, -value, value).astype(jnp.bfloat16)


def order_gradients_kernel(rows, rows_g):
    order = row_order(rows.shape[0], True, False)[rows.shape[0] // KINDS :]
    rows_g[...] = dot(order, rows[:, : rows_g.shape[1]]).astype(jnp.bfloat16)


def order_codes_kernel(rows, codes):
    count, width = rows.shape
    moved = dot(row_order(count, True, False), rows[...])
    codes[:, :width] = encode(moved[: count // KINDS])
    codes[:, width:] = encode(moved[count // KINDS :, width - TAIL :])


def restore_kernel(rows, restored):
    restored[...] = dot(row_order(rows.shape[0], False, True), rows[...]).astype(jnp.bfloat16)


def flat(rows):
    sources, count, width = rows.shape
    return rows.reshape(sources * count, width)


def forward_rows(codes, rows_g, weight_in, weight_out):
    width = weight_in.shape[0]
    decoded = decode(flat(codes[...]))
    rows_x = decoded[:, :width]
    rows_g = jnp.concatenate([flat(rows_g[...]), decoded[:, width:]], axis=1)
    pre_act = dot(rows_x, weight_in[...])
    hidden_grad = dot(rows_g, weight_out[...], ((1,), (1,)))
    value, slope = gelu_and_slope(pre_act)
    return rows_x, rows_g, value.astype(jnp.bfloat16), (hidden_grad * slope).astype(jnp.bfloat16)


def expert_kernel(group_ref, codes, rows_g, weight_in, weight_out, send):
    sources, part, _ = codes.shape
    width = send.shape[2]
    _, _, hidden, pre_grad = forward_rows(codes, rows_g, weight_in, weight_out)
    part_out = dot(hidden, weight_out[...]).astype(jnp.bfloat16)
    part_in = dot(pre_grad, weight_in[...], ((1,), (1,))).astype(jnp.bfloat16)
    narrow = KINDS * part
    own = pl.multiple_of(group_ref[0] * narrow, narrow)
    other = pl.multiple_of((EGRP - 1 - group_ref[0]) * narrow, narrow)
    send[:, pl.ds(other, narrow), :] = jnp.zeros((sources, narrow, width), jnp.bfloat16)
    send[:, pl.ds(own, part), :] = part_out.reshape(sources, part, width)
    send[:, pl.ds(own + part, part), :] = part_in.reshape(sources, part, width)


def weights_kernel(group_ref, codes, rows_g, weight_in, weight_out, grad_in, grad_out, sum_in, sum_out):
    rows_x, rows_g, hidden, pre_grad = forward_rows(codes, rows_g, weight_in, weight_out)

    @pl.when(pl.program_id(0) == 0)
    def _():
        sum_in[...] = jnp.zeros_like(sum_in)
        sum_out[...] = jnp.zeros_like(sum_out)

    sum_in[...] += dot(rows_x, pre_grad, ((0,), (0,)))
    sum_out[...] += dot(hidden, rows_g, ((0,), (0,)))

    @pl.when(pl.program_id(0) == pl.num_programs(0) - 1)
    def _():
        grad_in[...] = sum_in[...].astype(grad_in.dtype)
        grad_out[...] = sum_out[...].astype(grad_out.dtype)


def on_device(tokens, expert_ids, slot_ids, keep_mask, gate_prob, out_grad, in_weight, out_weight):
    tok_rows, width = tokens.shape
    intra_size = lax.axis_size("intra")
    inter_size = lax.axis_size("inter")
    blocks_ff = inter_size // EGRP
    group = (lax.axis_index("inter") // blocks_ff).astype(jnp.int32).reshape(1)
    weight_in = in_weight[0, 0]
    weight_out = out_weight[0, 0]
    hidden_units = weight_in.shape[1]
    wide = intra_size * TILE
    params = pltpu.CompilerParams(vmem_limit_bytes=VMEM_BYTES)
    small = pltpu.CompilerParams(vmem_limit_bytes=VMEM_SMALL)
    routing = (expert_ids[None], slot_ids[None], keep_mask[None], gate_prob[None])

    columns = width // 2
    some = lambda rows: pl.BlockSpec((rows, columns), lambda i: (0, i))
    one_row = pl.BlockSpec((1, tok_rows), lambda i: (0, 0))
    placed = pl.pallas_call(
        functools.partial(place_kernel, intra_size),
        grid=(width // columns,),
        in_specs=[some(tok_rows)] + [one_row] * 4 + [some(tok_rows)],
        out_specs=some(wide),
        out_shape=jax.ShapeDtypeStruct((wide, width), jnp.bfloat16),
        compiler_params=params,
        name="place",
    )(tokens, *routing, out_grad)
    moved = lax.all_to_all(placed.reshape(intra_size, TILE, width), "intra", 0, 0, tiled=True)
    part = wide // (EGRP * KINDS)
    half = EGRP * part

    def order(kernel, name, columns, dtype):
        return pl.pallas_call(
            kernel,
            out_shape=jax.ShapeDtypeStruct((half, columns), dtype),
            compiler_params=small,
            name=name,
        )(moved.reshape(wide, width))

    ordered_g = order(order_gradients_kernel, "order_gradients", width - TAIL, jnp.bfloat16)
    ordered_x = order(order_codes_kernel, "order_codes", width + TAIL, jnp.int16)
    spread_g = lax.all_gather(ordered_g[None], "inter", axis=0, tiled=True)
    spread_x = lax.all_gather(ordered_x[None], "inter", axis=0, tiled=True)

    step = 4
    whole = lambda i, group_ref: (0, 0)
    by_plane = pl.BlockSpec((step, wide, width), lambda i, group_ref: (i, 0, 0))
    own = lambda columns: pl.BlockSpec((step, part, columns), lambda i, group_ref: (i, group_ref[0], 0))
    in_block = pl.BlockSpec((width, hidden_units), whole)
    out_block = pl.BlockSpec((hidden_units, width), whole)

    def over_planes(kernel, name, out_specs, out_shape, scratch, grant=VMEM_BYTES):
        return pl.pallas_call(
            kernel,
            grid_spec=pltpu.PrefetchScalarGridSpec(
                num_scalar_prefetch=1,
                grid=(inter_size // step,),
                in_specs=[own(width + TAIL), own(width - TAIL), in_block, out_block],
                out_specs=out_specs,
                scratch_shapes=scratch,
            ),
            out_shape=out_shape,
            compiler_params=pltpu.CompilerParams(vmem_limit_bytes=grant),
            name=name,
        )(group, spread_x, spread_g, weight_in, weight_out)

    send = over_planes(
        expert_kernel, "expert", by_plane, jax.ShapeDtypeStruct((inter_size, wide, width), jnp.bfloat16), [], VMEM_MOST
    )
    summed = lax.psum_scatter(send, "inter", scatter_dimension=0, tiled=True)
    in_weight_grad, out_weight_grad = over_planes(
        weights_kernel,
        "weight_grads",
        [in_block, out_block],
        [jax.ShapeDtypeStruct(w.shape, jnp.bfloat16) for w in (weight_in, weight_out)],
        [pltpu.VMEM(w.shape, jnp.float32) for w in (weight_in, weight_out)],
    )
    summed, out_weight_grad, in_weight_grad = lax.optimization_barrier((summed, out_weight_grad, in_weight_grad))

    back = pl.pallas_call(
        restore_kernel,
        out_shape=jax.ShapeDtypeStruct((wide, width), jnp.bfloat16),
        compiler_params=small,
        name="restore",
    )(summed.reshape(wide, width))
    home = lax.all_to_all(back.reshape(intra_size, TILE, width), "intra", 0, 0, tiled=True)
    expert_out, gate_grad, token_grad = pl.pallas_call(
        functools.partial(pick_kernel, intra_size),
        out_shape=[
            jax.ShapeDtypeStruct((tok_rows, width), jnp.bfloat16),
            jax.ShapeDtypeStruct((1, tok_rows), jnp.float32),
            jax.ShapeDtypeStruct((tok_rows, width), jnp.bfloat16),
        ],
        compiler_params=small,
        name="pick",
    )(home.reshape(wide, width), *routing, out_grad)
    return (
        expert_out,
        gate_grad.reshape(tok_rows),
        token_grad,
        in_weight_grad[None, None],
        out_weight_grad[None, None],
    )


def solution(mesh):
    tok = P(("inter", "intra"), None)
    per = P(("inter", "intra"))
    wgt = P("inter", "intra", None, None)
    return jax.shard_map(
        on_device,
        mesh=mesh,
        in_specs=(tok, per, per, per, per, tok, wgt, wgt),
        out_specs=(tok, per, tok, wgt, wgt),
        check_vma=False,
    )
```
